32 devices in a mesh: depth: 4 (over y, core), slab: 8 (over z, x).
Axes of the slice: x: 2, y: 2, z: 4, core: 2. Of those that a mesh axis runs over, the one named last changes fastest.
Arguments:
- slabs: float32 [4, 8, 4, 256, 256], P('depth', 'slab'), as said below
- incident: float32 [4, 2048, 256], P('depth', 'slab'), may hold values from -6 to 6
Outputs:
- down_field: float32 [4, 2048, 256], P('depth', 'slab')
- reflected: float32 [4, 2048, 256], P('depth', 'slab')
The draws below stay inside these ranges and needn't reach their ends.
Inputs may be any that keep to these rules, and one draw needn't show every extreme that they name: Reflection blocks have spectral norm below one half; transmission blocks have spectral norm below 2, and every star product of consecutive slabs within a group has reflection blocks of norm below one.
All inputs are finite; a program needn't handle non-finite values.
Results may differ from the reference program's by a relative error of at most 0.0003.
Values sent between devices are 32-bit elements; how exact they have to be, the bound alone decides.
No kernel may reach another device: no remote copies, remote signals or barrier semaphores. Data moves between devices by JAX's collectives and lax.ppermute only.
A program may use at most 64 MiB of HBM per device.

```python
import jax
import jax.numpy as jnp
from jax import lax

M = 256
GROUPS = 4
SLABS = 8
SOURCES = 2048


def draw_slabs(key, part):
    keys = jax.random.split(jax.random.fold_in(key, 71), 6)
    shape = (GROUPS, SLABS, M, M)
    noise = [jnp.clip(jax.random.normal(keys[i], shape, jnp.float32), -4.0, 4.0) for i in range(4)]
    low = 0.88
    high = 0.99
    scale = M ** (-0.5)
    eye = jnp.eye(M, dtype=jnp.float32)
    diag_down = jnp.exp(jax.random.uniform(keys[4], (GROUPS, SLABS, M, 1), jnp.float32, jnp.log(low), jnp.log(high)))
    diag_up = jnp.exp(jax.random.uniform(keys[5], (GROUPS, SLABS, M, 1), jnp.float32, jnp.log(low), jnp.log(high)))
    refl = 0.1 * scale * noise[0]
    trans = eye * diag_down + 0.25 * scale * noise[1]
    back = 0.1 * scale * noise[2]
    upward = eye * diag_up + 0.25 * scale * noise[3]
    return jnp.stack([refl, trans, back, upward], axis=2)


def block_levels(stream_key, extent, cuts, low, high):
    gain = 1.0
    for position, blocks in cuts:
        draws = jax.random.uniform(jax.random.fold_in(jax.random.fold_in(stream_key, 6), position), (blocks,), jnp.float32, low / len(cuts), high / len(cuts))
        gain = gain * jnp.repeat(jnp.exp(draws), extent[position] // blocks).reshape((-1,) + (1,) * (len(extent) - 1 - position))
    return gain


def scatter_about(stream_key, shape, width, reach, cuts=(), held_as=jnp.bfloat16):
    result = jax.random.normal(stream_key, shape, jnp.float32) * width
    if len(cuts) > 0:
        result = block_levels(stream_key, shape, cuts, -0.22, 0.18) * result
    return jnp.clip(result, min=-reach, max=reach).astype(held_as)


def setup_inputs(seed: int = 0) -> dict:
    arg_keys = jax.random.split(jax.random.key(seed), 3)
    return {
        "slabs": draw_slabs(jax.random.fold_in(arg_keys[2], 71), 0),
        "incident": scatter_about(arg_keys[1], (GROUPS, SOURCES, M), 1.0, 6.0, ((0, 4), (1, 8)), jnp.float32),
    }


def matmul(left, right):
    return jnp.dot(left.astype(jnp.float32), right.astype(jnp.float32), precision=lax.Precision.HIGHEST, preferred_element_type=jnp.float32)

def times_transpose(rows, matrix):
    return lax.dot_general(rows.astype(jnp.float32), matrix.astype(jnp.float32), (((1,), (1,)), ((), ())), precision=lax.Precision.HIGHEST, preferred_element_type=jnp.float32)

def star(upper, lower):
    order = upper.shape[1]
    refl_a, trans_a, back_a, up_a = (upper[0], upper[1], upper[2], upper[3])
    refl_b, trans_b, back_b, up_b = (lower[0], lower[1], lower[2], lower[3])
    eye = jnp.eye(order, dtype=jnp.float32)
    system = eye - matmul(back_a, refl_b)
    right = jnp.concatenate([trans_a, matmul(back_a, up_b)], axis=1)
    solved = jnp.linalg.solve(system, right)
    first = solved[:, :order]
    second = solved[:, order:]
    refl = refl_a + matmul(up_a, matmul(refl_b, first))
    trans = matmul(trans_b, first)
    back = back_b + matmul(trans_b, second)
    upward = matmul(up_a, up_b + matmul(refl_b, second))
    return jnp.stack([refl, trans, back, upward])

def merge_group(group_slabs):

    def fold(index, carry):
        return star(carry, group_slabs[index])
    return lax.fori_loop(1, group_slabs.shape[0], fold, group_slabs[0])

def reference(slabs, incident):
    merged = lax.map(merge_group, slabs)

    def descend(arriving, items):
        blocks, injected = items
        field = injected + arriving
        return (times_transpose(field, blocks[1]), (field, times_transpose(field, blocks[0])))
    start = jnp.zeros(incident.shape[1:], jnp.float32)
    last, outs = lax.scan(descend, start, (merged, incident))
    return (outs[0], outs[1])
```

```python
import functools

import jax
import jax.numpy as jnp
from jax import lax
from jax.experimental import pallas as pl
from jax.experimental.pallas import tpu as pltpu
from jax.sharding import PartitionSpec as P

AXES = ("depth", "slab")


def split(value):
    high = value.astype(jnp.bfloat16)
    return high, (value - high.astype(jnp.float32)).astype(jnp.bfloat16)


def product(left, right):
    left_high, left_low = split(left)
    right_high, right_low = split(right)
    dot = functools.partial(jnp.dot, preferred_element_type=jnp.float32)
    return dot(left_high, right_high) + (dot(left_high, right_low) + dot(left_low, right_high))


def inverse(coupling, power, total):
    order = coupling.shape[0]
    row = lax.broadcasted_iota(jnp.int32, (order, order), 0)
    column = lax.broadcasted_iota(jnp.int32, (order, order), 1)
    result = coupling + jnp.where(row == column, 1.0, 0.0)
    for _ in range(2):
        coupling = product(coupling, coupling)
        result = result + product(result, coupling)
    power[...] = coupling
    total[...] = result

    def more(state):
        turn, size = state
        return jnp.logical_and(turn < 40, size > 2.0**-24)

    def step(state):
        turn, _ = state
        squared = product(power[...], power[...])
        total[...] += product(total[...], squared)
        power[...] = squared
        return turn + 1, jnp.sum(squared * squared)

    lax.while_loop(more, step, (0, jnp.sum(coupling * coupling)))
    return total[...]


def call(body, flags, blocks, outs, scratch=True):
    order = blocks[0].shape[-1]
    square = jax.ShapeDtypeStruct((order, order), jnp.float32)
    vmem = pl.BlockSpec(memory_space=pltpu.VMEM)
    results = pl.pallas_call(
        body,
        out_shape=[square] * outs,
        in_specs=[pl.BlockSpec(memory_space=pltpu.SMEM)] + [vmem] * len(blocks),
        out_specs=[vmem] * outs,
        scratch_shapes=[pltpu.VMEM((order, order), jnp.float32)] * 2 if scratch else [],
        compiler_params=pltpu.CompilerParams(vmem_limit_bytes=32 * 2**20),
    )(flags, *blocks)
    return list(results)


def first_step(flags, own, c0, out0, down, back, up, power, total):
    turned = 2 * flags[0]
    refl, trans, behind, upward = own[turned], own[1 + turned], own[2 - turned], own[3 - turned]
    solver = inverse(product(behind, c0[...]), power, total)
    down[...] = product(solver, trans)
    back[...] = product(solver, behind)
    bounce = product(upward, c0[...])
    up[...] = upward + product(bounce, back[...])
    out0[...] = refl + product(bounce, down[...])


def second_step(flags, down, back, c1, out1, through):
    out1[...] = product(c1[...], down[...])
    through[...] = product(c1[...], back[...])


def third_step(flags, up, through, c2, out2, rest):
    out2[...] = product(up[...], c2[...])
    rest[...] = product(through[...], c2[...])


def real_blocks(turned, blocks):
    return [jnp.where(turned, blocks[3 - i][...], blocks[i][...]) for i in range(4)]


def lower_run(flags, o0, o1, o2, o3, refl_b, trans_b, refl, trans, power, total):
    refl_a, trans_a, up_a, back_a = real_blocks(flags[0] == 1, (o0, o1, o2, o3))
    solver = inverse(product(back_a, refl_b[...]), power, total)
    down = product(solver, trans_a)
    refl[...] = refl_a + product(product(up_a, refl_b[...]), down)
    trans[...] = product(trans_b[...], down)


def star_into(upper, lower, refl, trans, up, back, power, total):
    refl_a, trans_a, up_a, back_a = upper
    refl_b, trans_b, up_b, back_b = lower
    solver = inverse(product(back_a, refl_b), power, total)
    down = product(solver, trans_a)
    bounce = product(up_a, refl_b)
    turned_up = product(solver, product(back_a, up_b))
    back[...] = back_b + product(trans_b, turned_up)
    trans[...] = product(trans_b, down)
    up[...] = product(up_a, up_b) + product(bounce, turned_up)
    refl[...] = refl_a + product(bounce, down)


def upper_run(flags, o0, o1, o2, o3, c0, c1, c2, c3, *outs):
    upper = real_blocks(flags[1] == 1, (c0, c1, c2, c3))
    lower = real_blocks(flags[0] == 1, (o0, o1, o2, o3))
    star_into(upper, lower, *outs)


def any_run(flags, o0, o1, o2, o3, c0, c1, c2, c3, *outs):
    own = real_blocks(flags[0] == 1, (o0, o1, o2, o3))
    came = real_blocks(flags[1] == 1, (c0, c1, c2, c3))
    below = flags[2] == 1
    upper = [jnp.where(below, c, o) for o, c in zip(own, came)]
    lower = [jnp.where(below, o, c) for o, c in zip(own, came)]
    star_into(upper, lower, *outs)


def whole_run(flags, refl_a, trans_a, up_a, back_a, refl_b, trans_b, refl, trans, power, total):
    solver = inverse(product(back_a[...], refl_b[...]), power, total)
    down = product(solver, trans_a[...])
    trans[...] = product(trans_b[...], down)
    refl[...] = refl_a[...] + product(product(up_a[...], refl_b[...]), down)


def times_transpose(rows, matrix):
    return lax.dot_general(
        rows, matrix, (((1,), (1,)), ((), ())), precision=lax.Precision.HIGH, preferred_element_type=jnp.float32
    )


def filled(useful, groups, count):
    def mate(device):
        return (device[0] ^ 1, device[1])

    devices = [(g, s) for g in range(groups) for s in range(count)]
    pairs = dict(useful)
    if groups % 2 == 0:
        targets = set(pairs.values())
        for device in devices:
            if device not in pairs and mate(device) not in targets:
                pairs[device] = mate(device)
        spare = set(devices) - set(pairs.values())
        for source, target in useful.items():
            if mate(target) not in pairs and mate(source) in spare:
                pairs[mate(target)] = mate(source)
                spare.discard(mate(source))
    return sorted((a[0] * count + a[1], b[0] * count + b[1]) for a, b in pairs.items())


def shards(slabs, incident):
    groups, count = lax.axis_size("depth"), lax.axis_size("slab")
    group, place = lax.axis_index("depth"), lax.axis_index("slab")
    levels = count.bit_length() - 1
    parity = group % 2

    def send(block, useful):
        return lax.ppermute(block, AXES, filled(useful, groups, count))

    def turn(g, k):
        return g % 2 if k < count // 2 - 1 else 0

    def home(g, k):
        return (g, 2 * k + turn(g, k))

    def guest(g, k):
        return (g, 2 * k + 1 - turn(g, k))

    pair = place // 2
    turned = jnp.where(pair == count // 2 - 1, 0, parity)
    owners = [range(count // 2)]
    merges = []
    while len(owners[-1]) > 1:
        now, kept = owners[-1], []
        merges.append([])
        for k in range(0, len(now), 2):
            below = len(now) > 2 and k // 2 % 2 == 0
            merges[-1].append((now[k], now[k + 1], True) if below else (now[k + 1], now[k], False))
            kept.append(merges[-1][-1][1])
        owners.append(kept)

    def routes(level, reverse=False, wanted=lambda merge: True):
        found = {}
        for merge in merges[level - 1]:
            source, target, _ = merge
            if wanted(merge):
                for g in range(groups):
                    a, b = home(g, source), home(g, target)
                    found[b if reverse else a] = a if reverse else b
        return found

    def is_one(pairs):
        return functools.reduce(jnp.logical_or, [pair == k for k in pairs], False)

    def flags(*values):
        return jnp.stack([jnp.asarray(v).astype(jnp.int32) for v in values])

    own = slabs[0, 0]
    spread = {guest(g, k): home(g, k) for g in range(groups) for k in range(count // 2)}
    came = []
    for index in (0, 1, 3, 2):
        chosen = lax.dynamic_index_in_dim(own, index + 2 * turned * (1 if index < 2 else -1), keepdims=False)
        came.append(send(chosen, spread))
    first = flags(turned)
    split_level = levels - 2
    onward = routes(1)
    onward_late = routes(1, wanted=lambda m: m[2]) if split_level == 1 else onward
    out0, down, back, up = call(first_step, first, [own, came[0]], 4)
    sent = [send(out0, onward)]
    out1, through = call(second_step, first, [down, back, came[1]], 2, False)
    sent.append(send(out1, onward))
    out2, rest = call(third_step, first, [up, through, came[2]], 2, False)
    sent.append(send(out2, onward_late))
    out3 = came[3] + rest
    sent.append(send(out3, onward_late))
    state = [out0, out1, out2, out3]
    own_turned, came_turned = turned, is_one([m[1] for m in merges[0] if m[0] < count // 2 - 1]) * parity

    for level in range(1, levels - 1):
        if level > 1:
            own_turned, came_turned = 0, 0
            late = routes(level, wanted=lambda m: m[2]) if level == split_level else routes(level)
            sent = [send(block, routes(level) if i < 2 else late) for i, block in enumerate(state)]
        if level < split_level:
            below = is_one([m[1] for m in merges[level - 1] if m[2]])
            state = call(any_run, flags(own_turned, came_turned, below), state + sent, 4)
        else:
            last = call(lower_run, flags(own_turned), state + sent[:2], 2)
            state = call(upper_run, flags(own_turned, came_turned), state + sent, 4)

    top = routes(levels - 1)
    arrived = [send(block, top) for block in last]
    refl, trans = call(whole_run, flags(0), state + arrived, 2)

    def spread_out(block):
        for level in range(levels - 1, 0, -1):
            fresh = is_one([m[0] for m in merges[level - 1]])
            block = jnp.where(fresh, send(block, routes(level, reverse=True)), block)
        at_home = place == 2 * pair + turned
        return jnp.where(at_home, block, send(block, {b: a for a, b in spread.items()}))

    trans = spread_out(trans)
    refl = spread_out(refl)

    injected = incident[0]
    field = injected
    for g in range(groups - 1):
        leaving = times_transpose(field, trans)
        arriving = send(leaving, {(g, s): (g + 1, s) for s in range(count)})
        field = jnp.where(group == g + 1, injected + arriving, field)
    bounced = times_transpose(field, refl)
    return (field[None], bounced[None])


def solution(mesh):
    placed = (P("depth", "slab", None, None, None), P("depth", "slab", None))
    return jax.shard_map(
        shards,
        mesh=mesh,
        in_specs=placed,
        out_specs=(P("depth", "slab", None), P("depth", "slab", None)),
        check_vma=False,
    )
```

```python
import functools

import jax
import jax.numpy as jnp
from jax import lax
from jax.experimental import pallas as pl
from jax.experimental.pallas import tpu as pltpu
from jax.sharding import PartitionSpec as P

AXES = ("depth", "slab")


def split(value):
    high = value.astype(jnp.bfloat16)
    return high, (value - high.astype(jnp.float32)).astype(jnp.bfloat16)


def product(left, right):
    left_high, left_low = split(left)
    right_high, right_low = split(right)
    dot = functools.partial(jnp.dot, preferred_element_type=jnp.float32)
    return dot(left_high, right_high) + (dot(left_high, right_low) + dot(left_low, right_high))


def inverse(coupling, power, total):
    order = coupling.shape[0]
    row = lax.broadcasted_iota(jnp.int32, (order, order), 0)
    column = lax.broadcasted_iota(jnp.int32, (order, order), 1)
    result = coupling + jnp.where(row == column, 1.0, 0.0)
    for _ in range(2):
        coupling = product(coupling, coupling)
        result = result + product(result, coupling)
    power[...] = coupling
    total[...] = result

    def more(state):
        turn, size = state
        return jnp.logical_and(turn < 40, size > 2.0**-24)

    def step(state):
        turn, _ = state
        squared = product(power[...], power[...])
        total[...] += product(total[...], squared)
        power[...] = squared
        return turn + 1, jnp.sum(squared * squared)

    lax.while_loop(more, step, (0, jnp.sum(coupling * coupling)))
    return total[...]


def call(body, flags, blocks, outs, scratch=True):
    order = blocks[0].shape[-1]
    square = jax.ShapeDtypeStruct((order, order), jnp.float32)
    vmem = pl.BlockSpec(memory_space=pltpu.VMEM)
    results = pl.pallas_call(
        body,
        out_shape=[square] * outs,
        in_specs=[pl.BlockSpec(memory_space=pltpu.SMEM)] + [vmem] * len(blocks),
        out_specs=[vmem] * outs,
        scratch_shapes=[pltpu.VMEM((order, order), jnp.float32)] * 2 if scratch else [],
        compiler_params=pltpu.CompilerParams(vmem_limit_bytes=32 * 2**20),
    )(flags, *blocks)
    return list(results)


def first_step(flags, own, c0, out0, down, back, up, power, total):
    turned = 2 * flags[0]
    refl, trans, behind, upward = own[turned], own[1 + turned], own[2 - turned], own[3 - turned]
    solver = inverse(product(behind, c0[...]), power, total)
    down[...] = product(solver, trans)
    back[...] = product(solver, behind)
    bounce = product(upward, c0[...])
    up[...] = upward + product(bounce, back[...])
    out0[...] = refl + product(bounce, down[...])


def second_step(flags, down, back, c1, out1, through):
    out1[...] = product(c1[...], down[...])
    through[...] = product(c1[...], back[...])


def third_step(flags, up, through, c2, out2, rest):
    out2[...] = product(up[...], c2[...])
    rest[...] = product(through[...], c2[...])


def real_blocks(turned, blocks):
    return [jnp.where(turned, blocks[3 - i][...], blocks[i][...]) for i in range(4)]


def lower_run(flags, o0, o1, o2, o3, refl_b, refl, down, power, total):
    refl_a, trans_a, up_a, back_a = real_blocks(flags[0] == 1, (o0, o1, o2, o3))
    solver = inverse(product(back_a, refl_b[...]), power, total)
    down[...] = product(solver, trans_a)
    refl[...] = refl_a + product(product(up_a, refl_b[...]), down[...])


def times(flags, left, right, out):
    out[...] = product(left[...], right[...])


def star_into(upper, lower, refl, trans, up, back, power, total):
    refl_a, trans_a, up_a, back_a = upper
    refl_b, trans_b, up_b, back_b = lower
    solver = inverse(product(back_a, refl_b), power, total)
    down = product(solver, trans_a)
    bounce = product(up_a, refl_b)
    turned_up = product(solver, product(back_a, up_b))
    back[...] = back_b + product(trans_b, turned_up)
    trans[...] = product(trans_b, down)
    up[...] = product(up_a, up_b) + product(bounce, turned_up)
    refl[...] = refl_a + product(bounce, down)


def upper_run(flags, o0, o1, o2, o3, c0, c1, c2, c3, *outs):
    upper = real_blocks(flags[1] == 1, (c0, c1, c2, c3))
    lower = real_blocks(flags[0] == 1, (o0, o1, o2, o3))
    star_into(upper, lower, *outs)


def any_run(flags, o0, o1, o2, o3, c0, c1, c2, c3, *outs):
    own = real_blocks(flags[0] == 1, (o0, o1, o2, o3))
    came = real_blocks(flags[1] == 1, (c0, c1, c2, c3))
    below = flags[2] == 1
    upper = [jnp.where(below, c, o) for o, c in zip(own, came)]
    lower = [jnp.where(below, o, c) for o, c in zip(own, came)]
    star_into(upper, lower, *outs)


def whole_run(flags, refl_a, trans_a, up_a, back_a, refl_b, refl, down, power, total):
    solver = inverse(product(back_a[...], refl_b[...]), power, total)
    down[...] = product(solver, trans_a[...])
    refl[...] = refl_a[...] + product(product(up_a[...], refl_b[...]), down[...])


def times_transpose(rows, matrix):
    return lax.dot_general(
        rows, matrix, (((1,), (1,)), ((), ())), precision=lax.Precision.HIGH, preferred_element_type=jnp.float32
    )


def filled(useful, groups, count):
    def mate(device):
        return (device[0] ^ 1, device[1])

    devices = [(g, s) for g in range(groups) for s in range(count)]
    pairs = dict(useful)
    if groups % 2 == 0:
        targets = set(pairs.values())
        for device in devices:
            if device not in pairs and mate(device) not in targets:
                pairs[device] = mate(device)
        spare = set(devices) - set(pairs.values())
        for source, target in useful.items():
            if mate(target) not in pairs and mate(source) in spare:
                pairs[mate(target)] = mate(source)
                spare.discard(mate(source))
    return sorted((a[0] * count + a[1], b[0] * count + b[1]) for a, b in pairs.items())


def shards(slabs, incident):
    groups, count = lax.axis_size("depth"), lax.axis_size("slab")
    group, place = lax.axis_index("depth"), lax.axis_index("slab")
    levels = count.bit_length() - 1
    parity = group % 2

    def send(block, useful):
        return lax.ppermute(block, AXES, filled(useful, groups, count))

    def turn(g, k):
        return g % 2 if k < count // 2 - 1 else 0

    def home(g, k):
        return (g, 2 * k + turn(g, k))

    def guest(g, k):
        return (g, 2 * k + 1 - turn(g, k))

    pair = place // 2
    turned = jnp.where(pair == count // 2 - 1, 0, parity)
    owners = [range(count // 2)]
    merges = []
    while len(owners[-1]) > 1:
        now, kept = owners[-1], []
        merges.append([])
        for k in range(0, len(now), 2):
            below = len(now) > 2 and k // 2 % 2 == 0
            merges[-1].append((now[k], now[k + 1], True) if below else (now[k + 1], now[k], False))
            kept.append(merges[-1][-1][1])
        owners.append(kept)

    def routes(level, reverse=False, wanted=lambda merge: True):
        found = {}
        for merge in merges[level - 1]:
            source, target, _ = merge
            if wanted(merge):
                for g in range(groups):
                    a, b = home(g, source), home(g, target)
                    found[b if reverse else a] = a if reverse else b
        return found

    def is_one(pairs):
        return functools.reduce(jnp.logical_or, [pair == k for k in pairs], False)

    def flags(*values):
        return jnp.stack([jnp.asarray(v).astype(jnp.int32) for v in values])

    own = slabs[0, 0]
    spread = {guest(g, k): home(g, k) for g in range(groups) for k in range(count // 2)}
    spread_late = {guest(g, k): home(g, k) for g in range(groups) for k in range(count // 2 - 1)}
    came, rest_of_own = [], own
    for index, wanted in ((0, spread), (1, spread), (3, spread_late), (2, spread_late)):
        chosen = lax.dynamic_index_in_dim(rest_of_own, index + 2 * turned * (1 if index < 2 else -1), keepdims=False)
        if not came:
            chosen, rest_of_own = lax.optimization_barrier((chosen, own))
        came.append(send(chosen, wanted))
    first = flags(turned)
    split_level = levels - 2
    onward = routes(1)
    onward_late = routes(1, wanted=lambda m: m[2]) if split_level == 1 else onward
    out0, down, back, up = call(first_step, first, [own, came[0]], 4)
    sent = [send(out0, onward)]
    out1, through = call(second_step, first, [down, back, came[1]], 2, False)
    sent.append(send(out1, onward))
    out2, rest = call(third_step, first, [up, through, came[2]], 2, False)
    sent.append(send(out2, onward_late))
    out3 = came[3] + rest
    sent.append(send(out3, onward_late))
    state = [out0, out1, out2, out3]
    own_turned, came_turned = turned, is_one([m[1] for m in merges[0] if m[0] < count // 2 - 1]) * parity

    for level in range(1, levels - 1):
        if level > 1:
            own_turned, came_turned = 0, 0
            late = routes(level, wanted=lambda m: m[2]) if level == split_level else routes(level)
            sent = [send(block, routes(level) if i < 2 else late) for i, block in enumerate(state)]
        if level < split_level:
            below = is_one([m[1] for m in merges[level - 1] if m[2]])
            state = call(any_run, flags(own_turned, came_turned, below), state + sent, 4)
        else:
            top = routes(levels - 1)
            low_refl, low_down = call(lower_run, flags(own_turned), state + sent[:1], 2)
            arrived = [send(low_refl, top)]
            (low_trans,) = call(times, flags(0), [sent[1], low_down], 1, False)
            arrived.append(send(low_trans, top))
            state = call(upper_run, flags(own_turned, came_turned), state + sent, 4)

    refl, down = call(whole_run, flags(0), state + arrived[:1], 2)
    (trans,) = call(times, flags(0), [arrived[1], down], 1, False)

    at_home = place == 2 * pair + turned
    hops = []
    for level in range(levels - 1, 0, -1):
        hops.append((is_one([m[0] for m in merges[level - 1]]), routes(level, reverse=True)))
    hops.append((jnp.logical_not(at_home), {b: a for a, b in spread.items()}))
    for i, (fresh, route) in enumerate(hops):
        trans = jnp.where(fresh, send(trans, route), trans)
        if i > 0:
            trans, _ = lax.optimization_barrier((trans, refl))
        refl = jnp.where(fresh, send(refl, route), refl)

    injected = incident[0]
    field = injected
    for g in range(groups - 1):
        leaving = times_transpose(field, trans)
        if g == 1:
            leaving, _ = lax.optimization_barrier((leaving, refl))
        arriving = send(leaving, {(g, s): (g + 1, s) for s in range(count)})
        field = jnp.where(group == g + 1, injected + arriving, field)
    bounced = times_transpose(field, refl)
    return (field[None], bounced[None])


def solution(mesh):
    placed = (P("depth", "slab", None, None, None), P("depth", "slab", None))
    return jax.shard_map(
        shards,
        mesh=mesh,
        in_specs=placed,
        out_specs=(P("depth", "slab", None), P("depth", "slab", None)),
        check_vma=False,
    )
```

```python
import functools

import jax
import jax.numpy as jnp
from jax import lax
from jax.experimental import pallas as pl
from jax.experimental.pallas import tpu as pltpu
from jax.sharding import PartitionSpec as P

AXES = ("depth", "slab")


def split(value):
    high = value.astype(jnp.bfloat16)
    return high, (value - high.astype(jnp.float32)).astype(jnp.bfloat16)


def product(left, right):
    left_high, left_low = split(left)
    right_high, right_low = split(right)
    dot = functools.partial(jnp.dot, preferred_element_type=jnp.float32)
    return dot(left_high, right_high) + (dot(left_high, right_low) + dot(left_low, right_high))


def inverse(coupling, power, total):
    order = coupling.shape[0]
    row = lax.broadcasted_iota(jnp.int32, (order, order), 0)
    column = lax.broadcasted_iota(jnp.int32, (order, order), 1)
    result = coupling + jnp.where(row == column, 1.0, 0.0)
    for _ in range(2):
        coupling = product(coupling, coupling)
        result = result + product(result, coupling)
    power[...] = coupling
    total[...] = result

    def more(state):
        turn, size = state
        return jnp.logical_and(turn < 40, size > 2.0**-24)

    def step(state):
        turn, _ = state
        squared = product(power[...], power[...])
        total[...] += product(total[...], squared)
        power[...] = squared
        return turn + 1, jnp.sum(squared * squared)

    lax.while_loop(more, step, (0, jnp.sum(coupling * coupling)))
    return total[...]


def call(body, blocks, outs, solves=False):
    order = blocks[0].shape[-1]
    square = jax.ShapeDtypeStruct((order, order), jnp.float32)
    vmem = pl.BlockSpec(memory_space=pltpu.VMEM)
    results = pl.pallas_call(
        body,
        out_shape=[square] * outs,
        in_specs=[vmem] * len(blocks),
        out_specs=[vmem] * outs,
        scratch_shapes=[pltpu.VMEM((order, order), jnp.float32)] * 2 if solves else [],
        compiler_params=pltpu.CompilerParams(vmem_limit_bytes=12 * 2**20),
    )(*blocks)
    return list(results)


def first_step(marks, own, c0, out0, down, back, up, power, total):
    turned = 2 * marks()[0]
    refl, trans, behind, upward = own[turned], own[1 + turned], own[2 - turned], own[3 - turned]
    solver = inverse(product(behind, c0[...]), power, total)
    down[...] = product(solver, trans)
    back[...] = product(solver, behind)
    bounce = product(upward, c0[...])
    up[...] = upward + product(bounce, back[...])
    out0[...] = refl + product(bounce, down[...])


def second_step(marks, down, back, up, c1, out1, kept):
    turned = marks()[0] == 1
    out1[...] = product(jnp.where(turned, up[...], c1[...]), jnp.where(turned, c1[...], down[...]))
    kept[...] = product(jnp.where(turned, back[...], c1[...]), jnp.where(turned, c1[...], back[...]))


def third_step(marks, down, up, kept, c2, out2, rest):
    turned = marks()[0] == 1
    out2[...] = product(jnp.where(turned, c2[...], up[...]), jnp.where(turned, down[...], c2[...]))
    rest[...] = product(jnp.where(turned, c2[...], kept[...]), jnp.where(turned, kept[...], c2[...]))


def ordered(turned, first, last):
    return jnp.where(turned, last[...], first[...]), jnp.where(turned, first[...], last[...])


def lower_run(marks, o0, o1, o2, o3, refl_b, refl, down, power, total):
    mark = marks()
    refl_a, back_a = ordered(mark[0] == 1, o0, o3)
    solver = inverse(product(back_a, refl_b[...]), power, total)
    down[...] = product(solver, o1[...])
    refl[...] = refl_a + product(product(o2[...], refl_b[...]), down[...])


def upper_run(marks, o0, o1, o2, o3, c0, c1, c3, back, trans, solver, power, total):
    mark = marks()
    refl_b, back_b = ordered(mark[0] == 1, o0, o3)
    _, back_a = ordered(mark[1] == 1, c0, c3)
    solver[...] = inverse(product(back_a, refl_b), power, total)
    through = product(o1[...], solver[...])
    back[...] = back_b + product(through, product(back_a, o2[...]))
    trans[...] = product(through, c1[...])


def whole_down(back_a, trans_a, refl_b, down, power, total):
    down[...] = product(inverse(product(back_a[...], refl_b[...]), power, total), trans_a[...])


def whole_refl(marks, o0, o2, o3, c0, c1, c2, c3, solver, low_refl, down, refl):
    mark = marks()
    refl_b, _ = ordered(mark[0] == 1, o0, o3)
    refl_a, back_a = ordered(mark[1] == 1, c0, c3)
    first = refl_a + product(c2[...], product(refl_b, product(solver[...], c1[...])))
    turned_up = product(solver[...], product(back_a, o2[...]))
    up = product(c2[...], o2[...] + product(refl_b, turned_up))
    refl[...] = first + product(up, product(low_refl[...], down[...]))


def any_run(marks, o0, o1, o2, o3, c0, c1, c2, c3, refl, trans, up, back, power, total):
    mark = marks()
    refl_own, back_own = ordered(mark[0] == 1, o0, o3)
    refl_came, back_came = ordered(mark[1] == 1, c0, c3)
    own, came = (refl_own, o1[...], o2[...], back_own), (refl_came, c1[...], c2[...], back_came)
    below = mark[2] == 1
    refl_a, trans_a, up_a, back_a = [jnp.where(below, c, o) for o, c in zip(own, came)]
    refl_b, trans_b, up_b, back_b = [jnp.where(below, o, c) for o, c in zip(own, came)]
    solver = inverse(product(back_a, refl_b), power, total)
    down = product(solver, trans_a)
    bounce = product(up_a, refl_b)
    turned_up = product(solver, product(back_a, up_b))
    back[...] = back_b + product(trans_b, turned_up)
    trans[...] = product(trans_b, down)
    up[...] = product(up_a, up_b) + product(bounce, turned_up)
    refl[...] = refl_a + product(bounce, down)


def times(left, right, out):
    out[...] = product(left[...], right[...])


def times_transpose(rows, matrix):
    return lax.dot_general(
        rows, matrix, (((1,), (1,)), ((), ())), precision=lax.Precision.HIGH, preferred_element_type=jnp.float32
    )


def filled(useful, groups, count):
    def mate(device):
        return (device[0] ^ 1, device[1])

    pairs = dict(useful)
    targets = set(pairs.values())
    devices = [(g, s) for g in range(groups) for s in range(count)]
    for device in devices:
        if device not in pairs and mate(device) not in targets:
            pairs[device] = mate(device)
    spare = set(devices) - set(pairs.values())
    for source, target in useful.items():
        if mate(target) not in pairs and mate(source) in spare:
            pairs[mate(target)] = mate(source)
            spare.discard(mate(source))
    return pairs


def shards(slabs, incident):
    groups, count = lax.axis_size("depth"), lax.axis_size("slab")
    group, place = lax.axis_index("depth"), lax.axis_index("slab")
    levels = count.bit_length() - 1
    parity = group % 2
    pair, side = place // 2, place % 2
    pairs = count // 2

    def send(block, useful, fill=True):
        route = filled(useful, groups, count) if fill else useful
        route = sorted((a[0] * count + a[1], b[0] * count + b[1]) for a, b in route.items())
        return lax.ppermute(block, AXES, route)

    def turn(g, k):
        return g % 2 if k < pairs - 1 else 0

    def home(g, k):
        return (g, 2 * k + turn(g, k))

    def guest(g, k):
        return (g, 2 * k + 1 - turn(g, k))

    turned = jnp.where(pair == pairs - 1, 0, parity)
    owners = [list(range(pairs))]
    merges = []
    while len(owners[-1]) > 1:
        now, kept = owners[-1], []
        merges.append([])
        for k in range(0, len(now), 2):
            below = len(now) > 2 and k // 2 % 2 == 0
            merges[-1].append((now[k], now[k + 1], True) if below else (now[k + 1], now[k], False))
            kept.append(merges[-1][-1][1])
        owners.append(kept)

    def routes(level, late=False):
        return {
            home(g, source): home(g, target)
            for source, target, below in merges[level - 1]
            if below or not late
            for g in range(groups)
        }

    def is_one(some):
        return functools.reduce(jnp.logical_or, [pair == k for k in some], False)

    def marks(level):
        odd, at = lax.axis_index("depth") % 2, lax.axis_index("slab") // 2

        def among(some):
            return functools.reduce(jnp.maximum, [(at == k).astype(jnp.int32) for k in some], jnp.int32(0))

        below = among([m[1] for m in merges[max(level, 1) - 1] if m[2]])
        if level > 1:
            return jnp.int32(0), jnp.int32(0), below
        return (1 - among([pairs - 1])) * odd, among([m[1] for m in merges[0] if m[0] < pairs - 1]) * odd, below

    own = slabs[0, 0]
    injected = incident[0]
    spread = {guest(g, k): home(g, k) for g in range(groups) for k in range(pairs)}
    spread_late = {guest(g, k): home(g, k) for g in range(groups) for k in range(pairs - 1)}
    chosen = lax.dynamic_index_in_dim(own, 2 * turned, keepdims=False)
    chosen, after = lax.optimization_barrier((chosen, own))
    came = [send(chosen, spread), send(after[1], spread), send(after[3], spread_late)]
    came.append(send(lax.dynamic_index_in_dim(after, 2 - 2 * turned, keepdims=False), spread_late))
    first = functools.partial(marks, 1)
    split_level = levels - 2
    late = split_level == 1
    out0, down, back, up = call(functools.partial(first_step, first), [own, came[0]], 4, True)
    sent = [send(out0, routes(1))]
    out1, kept = call(functools.partial(second_step, first), [down, back, up, came[1]], 2)
    sent.append(send(out1, routes(1)))
    out2, rest = call(functools.partial(third_step, first), [down, up, kept, came[2]], 2)
    sent.append(send(out2, routes(1, late)))
    out3 = came[3] + rest
    sent.append(send(out3, routes(1, late)))
    state = [out0, out1, out2, out3]
    for level in range(1, split_level):
        state = call(functools.partial(any_run, functools.partial(marks, level)), state + sent, 4, True)
        late = level + 1 == split_level
        sent = [send(block, routes(level + 1, late and i > 1)) for i, block in enumerate(state)]

    top = routes(levels - 1)
    split_marks = functools.partial(marks, split_level)
    low_refl, low_down = call(functools.partial(lower_run, split_marks), state + sent[:1], 2, True)
    low_refl = send(low_refl, top)
    (low_trans,) = call(times, [sent[1], low_down], 1)
    low_trans = send(low_trans, top)
    back_a, trans_a, solver = call(functools.partial(upper_run, split_marks), state + [sent[0], sent[1], sent[3]], 3, True)
    back_a, _ = lax.optimization_barrier((back_a, sent[2]))
    (down,) = call(whole_down, [back_a, trans_a, low_refl], 1, True)
    (trans,) = call(times, [low_trans, down], 1)
    (refl,) = call(functools.partial(whole_refl, split_marks), [state[0], state[2], state[3]] + sent + [solver, low_refl, down], 1)

    def line(g, k):
        return (g, 2 * k + g % 2)

    def hand_out(block):
        level = levels - 1
        while level > 0:
            steps = []
            for far, near, _ in merges[level - 1]:
                if level > 1:
                    below = {m[1]: m[0] for m in merges[level - 2]}
                    steps.append([(near, below[far]), (near, far), (near, below[near])])
                else:
                    steps.append([(near, far)])
            got = block
            for step in zip(*steps):
                fresh = is_one([target for _, target in step])
                route = {line(g, a): line(g, b) for a, b in step for g in range(groups)}
                got = jnp.where(fresh, send(block, route, False), got)
            block = got
            level -= 2
        return block

    trans, _ = lax.optimization_barrier((hand_out(trans), refl))
    refl = hand_out(refl)

    across = {}
    for g in range(groups):
        for k in range(pairs):
            across[line(g, k)] = (g | 1, 2 * k + 1 - g % 2)
    swap = {(g, s): (g ^ 1, s) for g in range(groups) for s in range(count)}
    crossed = send(trans, across, False)
    trans_even = jnp.where(side == 1, crossed, send(trans, swap))
    trans_odd = jnp.where(side == 1, trans, crossed)
    even = send(injected, swap)
    opposite = {line(g, k): (g, line(g, k)[1] ^ 1) for g in range(groups) for k in range(pairs)}
    spread_refl = jnp.where(side == parity, refl, send(refl, opposite))
    handed = jnp.zeros_like(injected)
    for j in range(0, groups, 2):
        field_even = even + handed
        field_odd = injected + times_transpose(field_even, trans_even)
        if j + 2 < groups:
            leaving, _ = lax.optimization_barrier((times_transpose(field_odd, trans_odd), refl))
            arriving = send(leaving, {(j + 1, s): (j + 3, s) for s in range(count)})
            arriving, _ = lax.optimization_barrier((arriving, spread_refl))
            handed = jnp.where(group // 2 == j // 2 + 1, arriving, handed)
    field = jnp.where(parity == 1, field_odd, send(field_even, swap))
    bounced = times_transpose(field, spread_refl)
    return (field[None], bounced[None])


def solution(mesh):
    placed = (P("depth", "slab", None, None, None), P("depth", "slab", None))
    return jax.shard_map(
        shards,
        mesh=mesh,
        in_specs=placed,
        out_specs=(P("depth", "slab", None), P("depth", "slab", None)),
        check_vma=False,
    )
```

```python
import functools

import jax
import jax.numpy as jnp
from jax import lax
from jax.experimental import pallas as pl
from jax.experimental.pallas import tpu as pltpu
from jax.sharding import PartitionSpec as P

AXES = ("depth", "slab")


def split(value):
    high = value.astype(jnp.bfloat16)
    return high, (value - high.astype(jnp.float32)).astype(jnp.bfloat16)


def product(left, right):
    left_high, left_low = split(left)
    right_high, right_low = split(right)
    dot = functools.partial(jnp.dot, preferred_element_type=jnp.float32)
    return dot(left_high, right_high) + (dot(left_high, right_low) + dot(left_low, right_high))


def inverse(coupling, power, total):
    order = coupling.shape[0]
    row = lax.broadcasted_iota(jnp.int32, (order, order), 0)
    column = lax.broadcasted_iota(jnp.int32, (order, order), 1)
    result = coupling + jnp.where(row == column, 1.0, 0.0)
    for _ in range(2):
        coupling = product(coupling, coupling)
        result = result + product(result, coupling)
    power[...] = coupling
    total[...] = result

    def more(state):
        turn, size = state
        return jnp.logical_and(turn < 40, size > 2.0**-24)

    def step(state):
        turn, _ = state
        squared = product(power[...], power[...])
        total[...] += product(total[...], squared)
        power[...] = squared
        return turn + 1, jnp.sum(squared * squared)

    lax.while_loop(more, step, (0, jnp.sum(coupling * coupling)))
    return total[...]


def call(body, blocks, outs, solves=False):
    order = blocks[0].shape[-1]
    square = jax.ShapeDtypeStruct((order, order), jnp.float32)
    vmem = pl.BlockSpec(memory_space=pltpu.VMEM)
    results = pl.pallas_call(
        body,
        out_shape=[square] * outs,
        in_specs=[vmem] * len(blocks),
        out_specs=[vmem] * outs,
        scratch_shapes=[pltpu.VMEM((order, order), jnp.float32)] * 2 if solves else [],
        compiler_params=pltpu.CompilerParams(vmem_limit_bytes=12 * 2**20),
    )(*blocks)
    return list(results)


def first_step(marks, own, c0, out0, down, solver, bounce, power, total):
    turned = 2 * marks()[0]
    refl, trans, behind, upward = own[turned], own[1 + turned], own[2 - turned], own[3 - turned]
    solver[...] = inverse(product(behind, c0[...]), power, total)
    down[...] = product(solver[...], trans)
    bounce[...] = product(upward, c0[...])
    out0[...] = refl + product(bounce[...], down[...])


def first_rest(marks, own, solver, bounce, back, up):
    turned = 2 * marks()[0]
    back[...] = product(solver[...], own[2 - turned])
    up[...] = own[3 - turned] + product(bounce[...], back[...])


def second_step(marks, down, back, up, c1, out1, kept):
    turned = marks()[0] == 1
    out1[...] = product(jnp.where(turned, up[...], c1[...]), jnp.where(turned, c1[...], down[...]))
    kept[...] = product(jnp.where(turned, back[...], c1[...]), jnp.where(turned, c1[...], back[...]))


def third_step(marks, down, up, kept, c2, out2, rest):
    turned = marks()[0] == 1
    out2[...] = product(jnp.where(turned, c2[...], up[...]), jnp.where(turned, down[...], c2[...]))
    rest[...] = product(jnp.where(turned, c2[...], kept[...]), jnp.where(turned, kept[...], c2[...]))


def ordered(turned, first, last):
    return jnp.where(turned, last[...], first[...]), jnp.where(turned, first[...], last[...])


def lower_run(marks, o0, o1, o2, o3, refl_b, refl, down, power, total):
    mark = marks()
    refl_a, back_a = ordered(mark[0] == 1, o0, o3)
    solver = inverse(product(back_a, refl_b[...]), power, total)
    down[...] = product(solver, o1[...])
    refl[...] = refl_a + product(product(o2[...], refl_b[...]), down[...])


def upper_run(marks, o0, o1, o2, o3, c0, c1, c3, back, trans, solver, power, total):
    mark = marks()
    refl_b, back_b = ordered(mark[0] == 1, o0, o3)
    _, back_a = ordered(mark[1] == 1, c0, c3)
    solver[...] = inverse(product(back_a, refl_b), power, total)
    through = product(o1[...], solver[...])
    back[...] = back_b + product(through, product(back_a, o2[...]))
    trans[...] = product(through, c1[...])


def whole_down(back_a, trans_a, refl_b, down, power, total):
    down[...] = product(inverse(product(back_a[...], refl_b[...]), power, total), trans_a[...])


def whole_refl(marks, o0, o2, o3, c0, c1, c2, c3, solver, low_refl, down, refl):
    mark = marks()
    refl_b, _ = ordered(mark[0] == 1, o0, o3)
    refl_a, back_a = ordered(mark[1] == 1, c0, c3)
    first = refl_a + product(c2[...], product(refl_b, product(solver[...], c1[...])))
    turned_up = product(solver[...], product(back_a, o2[...]))
    up = product(c2[...], o2[...] + product(refl_b, turned_up))
    refl[...] = first + product(up, product(low_refl[...], down[...]))


def any_run(marks, o0, o1, o2, o3, c0, c1, c2, c3, refl, trans, up, back, power, total):
    mark = marks()
    refl_own, back_own = ordered(mark[0] == 1, o0, o3)
    refl_came, back_came = ordered(mark[1] == 1, c0, c3)
    own, came = (refl_own, o1[...], o2[...], back_own), (refl_came, c1[...], c2[...], back_came)
    below = mark[2] == 1
    refl_a, trans_a, up_a, back_a = [jnp.where(below, c, o) for o, c in zip(own, came)]
    refl_b, trans_b, up_b, back_b = [jnp.where(below, o, c) for o, c in zip(own, came)]
    solver = inverse(product(back_a, refl_b), power, total)
    down = product(solver, trans_a)
    bounce = product(up_a, refl_b)
    turned_up = product(solver, product(back_a, up_b))
    back[...] = back_b + product(trans_b, turned_up)
    trans[...] = product(trans_b, down)
    up[...] = product(up_a, up_b) + product(bounce, turned_up)
    refl[...] = refl_a + product(bounce, down)


def times(left, right, out):
    out[...] = product(left[...], right[...])


def times_transpose(rows, matrix):
    return lax.dot_general(
        rows, matrix, (((1,), (1,)), ((), ())), precision=lax.Precision.HIGH, preferred_element_type=jnp.float32
    )


def filled(useful, groups, count):
    def mate(device):
        return (device[0] ^ 1, device[1])

    pairs = dict(useful)
    targets = set(pairs.values())
    devices = [(g, s) for g in range(groups) for s in range(count)]
    for device in devices:
        if device not in pairs and mate(device) not in targets:
            pairs[device] = mate(device)
    spare = set(devices) - set(pairs.values())
    for source, target in useful.items():
        if mate(target) not in pairs and mate(source) in spare:
            pairs[mate(target)] = mate(source)
            spare.discard(mate(source))
    return pairs


def shards(slabs, incident):
    groups, count = lax.axis_size("depth"), lax.axis_size("slab")
    group, place = lax.axis_index("depth"), lax.axis_index("slab")
    levels = count.bit_length() - 1
    parity = group % 2
    pair, side = place // 2, place % 2
    pairs = count // 2

    def send(block, useful, fill=True):
        route = filled(useful, groups, count) if fill else useful
        route = sorted((a[0] * count + a[1], b[0] * count + b[1]) for a, b in route.items())
        return lax.ppermute(block, AXES, route)

    def turn(g, k):
        return g % 2 if k < pairs - 1 else 0

    def home(g, k):
        return (g, 2 * k + turn(g, k))

    def guest(g, k):
        return (g, 2 * k + 1 - turn(g, k))

    turned = jnp.where(pair == pairs - 1, 0, parity)
    owners = [list(range(pairs))]
    merges = []
    while len(owners[-1]) > 1:
        now, kept = owners[-1], []
        merges.append([])
        for k in range(0, len(now), 2):
            below = len(now) > 2 and k // 2 % 2 == 0
            merges[-1].append((now[k], now[k + 1], True) if below else (now[k + 1], now[k], False))
            kept.append(merges[-1][-1][1])
        owners.append(kept)

    def routes(level, late=False):
        return {
            home(g, source): home(g, target)
            for source, target, below in merges[level - 1]
            if below or not late
            for g in range(groups)
        }

    def is_one(some):
        return functools.reduce(jnp.logical_or, [pair == k for k in some], False)

    def marks(level):
        odd, at = lax.axis_index("depth") % 2, lax.axis_index("slab") // 2

        def among(some):
            return functools.reduce(jnp.maximum, [(at == k).astype(jnp.int32) for k in some], jnp.int32(0))

        below = among([m[1] for m in merges[max(level, 1) - 1] if m[2]])
        if level > 1:
            return jnp.int32(0), jnp.int32(0), below
        return (1 - among([pairs - 1])) * odd, among([m[1] for m in merges[0] if m[0] < pairs - 1]) * odd, below

    own = slabs[0, 0]
    injected = incident[0]
    spread = {guest(g, k): home(g, k) for g in range(groups) for k in range(pairs)}
    spread_late = {guest(g, k): home(g, k) for g in range(groups) for k in range(pairs - 1)}
    chosen = lax.dynamic_index_in_dim(own, 2 * turned, keepdims=False)
    chosen, after = lax.optimization_barrier((chosen, own))
    came = [send(chosen, spread), send(after[1], spread), send(after[3], spread_late)]
    came.append(send(lax.dynamic_index_in_dim(after, 2 - 2 * turned, keepdims=False), spread_late))
    first = functools.partial(marks, 1)
    split_level = levels - 2
    late = split_level == 1
    out0, down, solver, bounce = call(functools.partial(first_step, first), [own, came[0]], 4, True)
    sent = [send(out0, routes(1))]
    back, up = call(functools.partial(first_rest, first), [own, solver, bounce], 2)
    out1, kept = call(functools.partial(second_step, first), [down, back, up, came[1]], 2)
    sent.append(send(out1, routes(1)))
    out2, rest = call(functools.partial(third_step, first), [down, up, kept, came[2]], 2)
    sent.append(send(out2, routes(1, late)))
    out3 = came[3] + rest
    sent.append(send(out3, routes(1, late)))
    state = [out0, out1, out2, out3]
    for level in range(1, split_level):
        state = call(functools.partial(any_run, functools.partial(marks, level)), state + sent, 4, True)
        late = level + 1 == split_level
        sent = [send(block, routes(level + 1, late and i > 1)) for i, block in enumerate(state)]

    top = routes(levels - 1)
    split_marks = functools.partial(marks, split_level)
    low_refl, low_down = call(functools.partial(lower_run, split_marks), state + sent[:1], 2, True)
    low_refl = send(low_refl, top)
    (low_trans,) = call(times, [sent[1], low_down], 1)
    low_trans = send(low_trans, top)
    back_a, trans_a, solver = call(functools.partial(upper_run, split_marks), state + [sent[0], sent[1], sent[3]], 3, True)
    back_a, _ = lax.optimization_barrier((back_a, sent[2]))
    (down,) = call(whole_down, [back_a, trans_a, low_refl], 1, True)
    (trans,) = call(times, [low_trans, down], 1)
    (refl,) = call(functools.partial(whole_refl, split_marks), [state[0], state[2], state[3]] + sent + [solver, low_refl, down], 1)

    def line(g, k):
        return (g, 2 * k + g % 2)

    def hand_out(block, fill):
        level = levels - 1
        while level > 0:
            steps = []
            for far, near, _ in merges[level - 1]:
                if level > 1:
                    below = {m[1]: m[0] for m in merges[level - 2]}
                    steps.append([(near, below[far]), (near, far), (near, below[near])])
                else:
                    steps.append([(near, far)])
            got = block
            for step in zip(*steps):
                fresh = is_one([target for _, target in step])
                route = {line(g, a): line(g, b) for a, b in step for g in range(groups)}
                got = jnp.where(fresh, send(block, route, fill), got)
            block = got
            level -= 2
        return block

    trans, _ = lax.optimization_barrier((hand_out(trans, True), refl))
    refl = hand_out(refl, False)

    across = {}
    for g in range(groups):
        for k in range(pairs):
            across[line(g, k)] = (g | 1, 2 * k + 1 - g % 2)
    swap = {(g, s): (g ^ 1, s) for g in range(groups) for s in range(count)}
    crossed = send(trans, across, False)
    trans_even = jnp.where(side == 1, crossed, send(trans, swap))
    trans_odd = jnp.where(side == 1, trans, crossed)
    even = send(injected, swap)
    opposite = {line(g, k): (g, line(g, k)[1] ^ 1) for g in range(groups) for k in range(pairs)}
    spread_refl = jnp.where(side == parity, refl, send(refl, opposite))
    handed = jnp.zeros_like(injected)
    for j in range(0, groups, 2):
        field_even = even + handed
        field_odd = injected + times_transpose(field_even, trans_even)
        if j + 2 < groups:
            leaving, _ = lax.optimization_barrier((times_transpose(field_odd, trans_odd), refl))
            arriving = send(leaving, {(j + 1, s): (j + 3, s) for s in range(count)})
            arriving, _ = lax.optimization_barrier((arriving, spread_refl))
            handed = jnp.where(group // 2 == j // 2 + 1, arriving, handed)
    field = jnp.where(parity == 1, field_odd, send(field_even, swap))
    bounced = times_transpose(field, spread_refl)
    return (field[None], bounced[None])


def solution(mesh):
    placed = (P("depth", "slab", None, None, None), P("depth", "slab", None))
    return jax.shard_map(
        shards,
        mesh=mesh,
        in_specs=placed,
        out_specs=(P("depth", "slab", None), P("depth", "slab", None)),
        check_vma=False,
    )
```

```python
import functools

import jax
import jax.numpy as jnp
from jax import lax
from jax.experimental import pallas as pl
from jax.experimental.pallas import tpu as pltpu
from jax.sharding import PartitionSpec as P

AXES = ("depth", "slab")


def split(value):
    high = value.astype(jnp.bfloat16)
    return high, (value - high.astype(jnp.float32)).astype(jnp.bfloat16)


def product(left, right):
    left_high, left_low = split(left)
    right_high, right_low = split(right)
    dot = functools.partial(jnp.dot, preferred_element_type=jnp.float32)
    return dot(left_high, right_high) + (dot(left_high, right_low) + dot(left_low, right_high))


def rough(left, right):
    return jnp.dot(left.astype(jnp.bfloat16), right.astype(jnp.bfloat16), preferred_element_type=jnp.float32)


def solve(coupling, use, power, total):
    order = coupling.shape[0]
    row = lax.broadcasted_iota(jnp.int32, (order, order), 0)
    column = lax.broadcasted_iota(jnp.int32, (order, order), 1)
    start = coupling + jnp.where(row == column, 1.0, 0.0)
    squared = product(coupling, coupling)
    power[...] = squared
    total[...] = start
    size = jnp.sum(squared * squared)
    result = start + (squared + rough(coupling, squared))
    use(result + rough(rough(squared, squared), result))

    @pl.when(size > 2.0**-10)
    def _():
        total[...] += product(total[...], power[...])

        def more(state):
            turn, last = state
            return jnp.logical_and(turn < 40, last > 2.0**-24)

        def step(state):
            turn, _ = state
            following = product(power[...], power[...])
            total[...] += product(total[...], following)
            power[...] = following
            return turn + 1, jnp.sum(following * following)

        lax.while_loop(more, step, (0, size))
        use(total[...])


def call(body, blocks, outs, solves=False):
    order = blocks[0].shape[-1]
    square = jax.ShapeDtypeStruct((order, order), jnp.float32)
    vmem = pl.BlockSpec(memory_space=pltpu.VMEM)
    results = pl.pallas_call(
        body,
        out_shape=[square] * outs,
        in_specs=[vmem] * len(blocks),
        out_specs=[vmem] * outs,
        scratch_shapes=[pltpu.VMEM((order, order), jnp.float32)] * 2 if solves else [],
        compiler_params=pltpu.CompilerParams(vmem_limit_bytes=12 * 2**20),
    )(*blocks)
    return list(results)


def first_step(marks, own, c0, out0, down, solver, bounce, power, total):
    turned = 2 * marks()[0]
    refl, trans, behind, upward = own[turned], own[1 + turned], own[2 - turned], own[3 - turned]
    bounce[...] = product(upward, c0[...])

    def use(value):
        solver[...] = value
        down[...] = product(value, trans)
        out0[...] = refl + product(bounce[...], down[...])

    solve(product(behind, c0[...]), use, power, total)


def first_rest(marks, own, solver, bounce, back, up):
    turned = 2 * marks()[0]
    back[...] = product(solver[...], own[2 - turned])
    up[...] = own[3 - turned] + product(bounce[...], back[...])


def second_step(marks, down, back, up, c1, out1, kept):
    turned = marks()[0] == 1
    out1[...] = product(jnp.where(turned, up[...], c1[...]), jnp.where(turned, c1[...], down[...]))
    kept[...] = product(jnp.where(turned, back[...], c1[...]), jnp.where(turned, c1[...], back[...]))


def third_step(marks, down, up, kept, c2, out2, rest):
    turned = marks()[0] == 1
    out2[...] = product(jnp.where(turned, c2[...], up[...]), jnp.where(turned, down[...], c2[...]))
    rest[...] = product(jnp.where(turned, c2[...], kept[...]), jnp.where(turned, kept[...], c2[...]))


def ordered(turned, first, last):
    return jnp.where(turned, last[...], first[...]), jnp.where(turned, first[...], last[...])


def lower_run(marks, o0, o1, o2, o3, refl_b, refl, down, power, total):
    refl_a, back_a = ordered(marks()[0] == 1, o0, o3)
    bounce = product(o2[...], refl_b[...])

    def use(value):
        down[...] = product(value, o1[...])
        refl[...] = refl_a + product(bounce, down[...])

    solve(product(back_a, refl_b[...]), use, power, total)


def upper_run(marks, o0, o1, o2, o3, c0, c1, c3, back, trans, solver, power, total):
    mark = marks()
    refl_b, back_b = ordered(mark[0] == 1, o0, o3)
    _, back_a = ordered(mark[1] == 1, c0, c3)
    turned_up = product(back_a, o2[...])

    def use(value):
        solver[...] = value
        through = product(o1[...], value)
        back[...] = back_b + product(through, turned_up)
        trans[...] = product(through, c1[...])

    solve(product(back_a, refl_b), use, power, total)


def whole_down(back_a, trans_a, refl_b, down, power, total):
    def use(value):
        down[...] = product(value, trans_a[...])

    solve(product(back_a[...], refl_b[...]), use, power, total)


def whole_refl(marks, o0, o2, o3, c0, c1, c2, c3, solver, low_refl, down, refl):
    mark = marks()
    refl_b, _ = ordered(mark[0] == 1, o0, o3)
    refl_a, back_a = ordered(mark[1] == 1, c0, c3)
    first = refl_a + product(c2[...], product(refl_b, product(solver[...], c1[...])))
    turned_up = product(solver[...], product(back_a, o2[...]))
    up = product(c2[...], o2[...] + product(refl_b, turned_up))
    refl[...] = first + product(up, product(low_refl[...], down[...]))


def any_run(marks, o0, o1, o2, o3, c0, c1, c2, c3, refl, trans, up, back, power, total):
    mark = marks()
    refl_own, back_own = ordered(mark[0] == 1, o0, o3)
    refl_came, back_came = ordered(mark[1] == 1, c0, c3)
    own, came = (refl_own, o1[...], o2[...], back_own), (refl_came, c1[...], c2[...], back_came)
    below = mark[2] == 1
    refl_a, trans_a, up_a, back_a = [jnp.where(below, c, o) for o, c in zip(own, came)]
    refl_b, trans_b, up_b, back_b = [jnp.where(below, o, c) for o, c in zip(own, came)]
    bounce = product(up_a, refl_b)

    def use(value):
        down = product(value, trans_a)
        turned_up = product(value, product(back_a, up_b))
        back[...] = back_b + product(trans_b, turned_up)
        trans[...] = product(trans_b, down)
        up[...] = product(up_a, up_b) + product(bounce, turned_up)
        refl[...] = refl_a + product(bounce, down)

    solve(product(back_a, refl_b), use, power, total)


def times(left, right, out):
    out[...] = product(left[...], right[...])


def times_transpose(rows, matrix):
    return lax.dot_general(
        rows, matrix, (((1,), (1,)), ((), ())), precision=lax.Precision.HIGH, preferred_element_type=jnp.float32
    )


def last_step(odd, even, refl, field_out, bounced_out, field, bounced, sems):
    field[...] = jnp.where(lax.axis_index("depth") % 2 == 1, odd[...], even[...])
    rows = pltpu.make_async_copy(field, field_out, sems.at[0])
    rows.start()
    half = field.shape[0] // 2
    matrix_high, matrix_low = split(refl[...])
    dot = functools.partial(
        lax.dot_general, dimension_numbers=(((1,), (1,)), ((), ())), preferred_element_type=jnp.float32
    )
    copies = []
    for i in range(2):
        part = pl.ds(i * half, half)
        high, low = split(field[part, :])
        bounced[part, :] = dot(high, matrix_high) + (dot(high, matrix_low) + dot(low, matrix_high))
        copies.append(pltpu.make_async_copy(bounced.at[part, :], bounced_out.at[part, :], sems.at[1 + i]))
        copies[-1].start()
    rows.wait()
    for copy in copies:
        copy.wait()


def finish(odd, even, refl):
    shape = jax.ShapeDtypeStruct(odd.shape, jnp.float32)
    vmem, hbm = pl.BlockSpec(memory_space=pltpu.VMEM), pl.BlockSpec(memory_space=pl.ANY)
    return pl.pallas_call(
        last_step,
        out_shape=[shape, shape],
        in_specs=[vmem] * 3,
        out_specs=[hbm, hbm],
        scratch_shapes=[pltpu.VMEM(odd.shape, jnp.float32)] * 2 + [pltpu.SemaphoreType.DMA((3,))],
        compiler_params=pltpu.CompilerParams(vmem_limit_bytes=12 * 2**20),
    )(odd, even, refl)


def filled(useful, groups, count):
    def mate(device):
        return (device[0] ^ 1, device[1])

    pairs = dict(useful)
    targets = set(pairs.values())
    devices = [(g, s) for g in range(groups) for s in range(count)]
    for device in devices:
        if device not in pairs and mate(device) not in targets:
            pairs[device] = mate(device)
    spare = set(devices) - set(pairs.values())
    for source, target in useful.items():
        if mate(target) not in pairs and mate(source) in spare:
            pairs[mate(target)] = mate(source)
            spare.discard(mate(source))
    return pairs


def shards(slabs, incident):
    groups, count = lax.axis_size("depth"), lax.axis_size("slab")
    group, place = lax.axis_index("depth"), lax.axis_index("slab")
    levels = count.bit_length() - 1
    parity = group % 2
    pair, side = place // 2, place % 2
    pairs = count // 2

    def send(block, useful, fill=True):
        route = filled(useful, groups, count) if fill else useful
        route = sorted((a[0] * count + a[1], b[0] * count + b[1]) for a, b in route.items())
        return lax.ppermute(block, AXES, route)

    def turn(g, k):
        return g % 2 if k < pairs - 1 else 0

    def home(g, k):
        return (g, 2 * k + turn(g, k))

    def guest(g, k):
        return (g, 2 * k + 1 - turn(g, k))

    turned = jnp.where(pair == pairs - 1, 0, parity)
    owners = [list(range(pairs))]
    merges = []
    while len(owners[-1]) > 1:
        now, kept = owners[-1], []
        merges.append([])
        for k in range(0, len(now), 2):
            below = len(now) > 2 and k // 2 % 2 == 0
            merges[-1].append((now[k], now[k + 1], True) if below else (now[k + 1], now[k], False))
            kept.append(merges[-1][-1][1])
        owners.append(kept)

    def routes(level, late=False):
        return {
            home(g, source): home(g, target)
            for source, target, below in merges[level - 1]
            if below or not late
            for g in range(groups)
        }

    def is_one(some):
        return functools.reduce(jnp.logical_or, [pair == k for k in some], False)

    def marks(level):
        odd, at = lax.axis_index("depth") % 2, lax.axis_index("slab") // 2

        def among(some):
            return functools.reduce(jnp.maximum, [(at == k).astype(jnp.int32) for k in some], jnp.int32(0))

        below = among([m[1] for m in merges[max(level, 1) - 1] if m[2]])
        if level > 1:
            return jnp.int32(0), jnp.int32(0), below
        return (1 - among([pairs - 1])) * odd, among([m[1] for m in merges[0] if m[0] < pairs - 1]) * odd, below

    own = slabs[0, 0]
    injected = incident[0]
    spread = {guest(g, k): home(g, k) for g in range(groups) for k in range(pairs)}
    spread_late = {guest(g, k): home(g, k) for g in range(groups) for k in range(pairs - 1)}
    chosen = lax.dynamic_index_in_dim(own, 2 * turned, keepdims=False)
    chosen, after = lax.optimization_barrier((chosen, own))
    came = [send(chosen, spread), send(after[1], spread), send(after[3], spread_late)]
    came.append(send(lax.dynamic_index_in_dim(after, 2 - 2 * turned, keepdims=False), spread_late))
    first = functools.partial(marks, 1)
    split_level = levels - 2
    late = split_level == 1
    out0, down, solver, bounce = call(functools.partial(first_step, first), [own, came[0]], 4, True)
    sent = [send(out0, routes(1))]
    back, up = call(functools.partial(first_rest, first), [own, solver, bounce], 2)
    out1, kept = call(functools.partial(second_step, first), [down, back, up, came[1]], 2)
    sent.append(send(out1, routes(1)))
    out2, rest = call(functools.partial(third_step, first), [down, up, kept, came[2]], 2)
    sent.append(send(out2, routes(1, late)))
    out3 = came[3] + rest
    sent.append(send(out3, routes(1, late)))
    state = [out0, out1, out2, out3]
    for level in range(1, split_level):
        state = call(functools.partial(any_run, functools.partial(marks, level)), state + sent, 4, True)
        late = level + 1 == split_level
        sent = [send(block, routes(level + 1, late and i > 1)) for i, block in enumerate(state)]

    top = routes(levels - 1)
    split_marks = functools.partial(marks, split_level)
    low_refl, low_down = call(functools.partial(lower_run, split_marks), state + sent[:1], 2, True)
    low_refl = send(low_refl, top)
    (low_trans,) = call(times, [sent[1], low_down], 1)
    low_trans = send(low_trans, top)
    back_a, trans_a, solver = call(functools.partial(upper_run, split_marks), state + [sent[0], sent[1], sent[3]], 3, True)
    back_a, _ = lax.optimization_barrier((back_a, sent[2]))
    (down,) = call(whole_down, [back_a, trans_a, low_refl], 1, True)
    (trans,) = call(times, [low_trans, down], 1)
    (refl,) = call(functools.partial(whole_refl, split_marks), [state[0], state[2], state[3]] + sent + [solver, low_refl, down], 1)

    def line(g, k):
        return (g, 2 * k + g % 2)

    def hand_out(block, fill):
        level = levels - 1
        while level > 0:
            steps = []
            for far, near, _ in merges[level - 1]:
                if level > 1:
                    below = {m[1]: m[0] for m in merges[level - 2]}
                    steps.append([(near, below[far]), (near, far), (near, below[near])])
                else:
                    steps.append([(near, far)])
            got = block
            for step, full in zip(zip(*steps), fill):
                fresh = is_one([target for _, target in step])
                route = {line(g, a): line(g, b) for a, b in step for g in range(groups)}
                got = jnp.where(fresh, send(block, route, full), got)
            block = got
            level -= 2
        return block

    trans, _ = lax.optimization_barrier((hand_out(trans, (True, True, False)), refl))
    refl = hand_out(refl, (False, False, False))

    across = {}
    for g in range(groups):
        for k in range(pairs):
            across[line(g, k)] = (g | 1, 2 * k + 1 - g % 2)
    swap = {(g, s): (g ^ 1, s) for g in range(groups) for s in range(count)}
    crossed = send(trans, across, False)
    trans_even = jnp.where(side == 1, crossed, send(trans, swap))
    trans_odd = jnp.where(side == 1, trans, crossed)
    even = send(injected, swap)
    opposite = {line(g, k): (g, line(g, k)[1] ^ 1) for g in range(groups) for k in range(pairs)}
    spread_refl = jnp.where(side == parity, refl, send(refl, opposite))
    handed = jnp.zeros_like(injected)
    for j in range(0, groups, 2):
        field_even = even + handed
        field_odd = injected + times_transpose(field_even, trans_even)
        if j + 2 < groups:
            leaving, _ = lax.optimization_barrier((times_transpose(field_odd, trans_odd), refl))
            arriving = send(leaving, {(j + 1, s): (j + 3, s) for s in range(count)})
            arriving, _ = lax.optimization_barrier((arriving, spread_refl))
            handed = jnp.where(group // 2 == j // 2 + 1, arriving, handed)
    field, bounced = finish(field_odd, send(field_even, swap), spread_refl)
    return (field[None], bounced[None])


def solution(mesh):
    placed = (P("depth", "slab", None, None, None), P("depth", "slab", None))
    return jax.shard_map(
        shards,
        mesh=mesh,
        in_specs=placed,
        out_specs=(P("depth", "slab", None), P("depth", "slab", None)),
        check_vma=False,
    )
```

```python
import functools

import jax
import jax.numpy as jnp
from jax import lax
from jax.experimental import pallas as pl
from jax.experimental.pallas import tpu as pltpu
from jax.sharding import PartitionSpec as P

AXES = ("depth", "slab")


def split(value):
    high = value.astype(jnp.bfloat16)
    return high, (value - high.astype(jnp.float32)).astype(jnp.bfloat16)


def product(left, right):
    left_high, left_low = split(left)
    right_high, right_low = split(right)
    dot = functools.partial(jnp.dot, preferred_element_type=jnp.float32)
    return dot(left_high, right_high) + (dot(left_high, right_low) + dot(left_low, right_high))


def rough(left, right):
    return jnp.dot(left.astype(jnp.bfloat16), right.astype(jnp.bfloat16), preferred_element_type=jnp.float32)


def solve(coupling, use, power, total):
    order = coupling.shape[0]
    row = lax.broadcasted_iota(jnp.int32, (order, order), 0)
    column = lax.broadcasted_iota(jnp.int32, (order, order), 1)
    start = coupling + jnp.where(row == column, 1.0, 0.0)
    squared = product(coupling, coupling)
    power[...] = squared
    total[...] = start
    size = jnp.sum(squared * squared)
    result = start + (squared + rough(coupling, squared))
    use(result + rough(rough(squared, squared), result))

    @pl.when(size > 2.0**-10)
    def _():
        total[...] += product(total[...], power[...])

        def more(state):
            turn, last = state
            return jnp.logical_and(turn < 40, last > 2.0**-24)

        def step(state):
            turn, _ = state
            following = product(power[...], power[...])
            total[...] += product(total[...], following)
            power[...] = following
            return turn + 1, jnp.sum(following * following)

        lax.while_loop(more, step, (0, size))
        use(total[...])


def call(body, blocks, outs, solves=False):
    order = blocks[0].shape[-1]
    square = jax.ShapeDtypeStruct((order, order), jnp.float32)
    vmem = pl.BlockSpec(memory_space=pltpu.VMEM)
    results = pl.pallas_call(
        body,
        out_shape=[square] * outs,
        in_specs=[vmem] * len(blocks),
        out_specs=[vmem] * outs,
        scratch_shapes=[pltpu.VMEM((order, order), jnp.float32)] * 2 if solves else [],
        compiler_params=pltpu.CompilerParams(vmem_limit_bytes=12 * 2**20),
    )(*blocks)
    return list(results)


def first_step(marks, own, c0, out0, down, solver, bounce, power, total):
    turned = 2 * marks()[0]
    refl, trans, behind, upward = own[turned], own[1 + turned], own[2 - turned], own[3 - turned]
    bounce[...] = product(upward, c0[...])

    def use(value):
        solver[...] = value
        down[...] = product(value, trans)
        out0[...] = refl + product(bounce[...], down[...])

    solve(product(behind, c0[...]), use, power, total)


def first_rest(marks, own, solver, bounce, back, up):
    turned = 2 * marks()[0]
    back[...] = product(solver[...], own[2 - turned])
    up[...] = own[3 - turned] + product(bounce[...], back[...])


def second_step(marks, down, back, up, c1, out1, kept):
    turned = marks()[0] == 1
    out1[...] = product(jnp.where(turned, up[...], c1[...]), jnp.where(turned, c1[...], down[...]))
    kept[...] = product(jnp.where(turned, back[...], c1[...]), jnp.where(turned, c1[...], back[...]))


def third_step(marks, down, up, kept, c2, out2, rest):
    turned = marks()[0] == 1
    out2[...] = product(jnp.where(turned, c2[...], up[...]), jnp.where(turned, down[...], c2[...]))
    rest[...] = product(jnp.where(turned, c2[...], kept[...]), jnp.where(turned, kept[...], c2[...]))


def ordered(turned, first, last):
    return jnp.where(turned, last[...], first[...]), jnp.where(turned, first[...], last[...])


def lower_run(marks, o0, o1, o2, o3, refl_b, refl, down, power, total):
    refl_a, back_a = ordered(marks()[0] == 1, o0, o3)
    bounce = product(o2[...], refl_b[...])

    def use(value):
        down[...] = product(value, o1[...])
        refl[...] = refl_a + product(bounce, down[...])

    solve(product(back_a, refl_b[...]), use, power, total)


def upper_run(marks, o0, o1, o2, o3, c0, c1, c3, back, trans, solver, power, total):
    mark = marks()
    refl_b, back_b = ordered(mark[0] == 1, o0, o3)
    _, back_a = ordered(mark[1] == 1, c0, c3)
    turned_up = product(back_a, o2[...])

    def use(value):
        solver[...] = value
        through = product(o1[...], value)
        back[...] = back_b + product(through, turned_up)
        trans[...] = product(through, c1[...])

    solve(product(back_a, refl_b), use, power, total)


def whole_down(back_a, trans_a, refl_b, down, power, total):
    def use(value):
        down[...] = product(value, trans_a[...])

    solve(product(back_a[...], refl_b[...]), use, power, total)


def whole_refl(marks, o0, o2, o3, c0, c1, c2, c3, solver, low_refl, down, refl):
    mark = marks()
    refl_b, _ = ordered(mark[0] == 1, o0, o3)
    refl_a, back_a = ordered(mark[1] == 1, c0, c3)
    first = refl_a + product(c2[...], product(refl_b, product(solver[...], c1[...])))
    turned_up = product(solver[...], product(back_a, o2[...]))
    up = product(c2[...], o2[...] + product(refl_b, turned_up))
    refl[...] = first + product(up, product(low_refl[...], down[...]))


def any_run(marks, o0, o1, o2, o3, c0, c1, c2, c3, refl, trans, up, back, power, total):
    mark = marks()
    refl_own, back_own = ordered(mark[0] == 1, o0, o3)
    refl_came, back_came = ordered(mark[1] == 1, c0, c3)
    own, came = (refl_own, o1[...], o2[...], back_own), (refl_came, c1[...], c2[...], back_came)
    below = mark[2] == 1
    refl_a, trans_a, up_a, back_a = [jnp.where(below, c, o) for o, c in zip(own, came)]
    refl_b, trans_b, up_b, back_b = [jnp.where(below, o, c) for o, c in zip(own, came)]
    bounce = product(up_a, refl_b)

    def use(value):
        down = product(value, trans_a)
        turned_up = product(value, product(back_a, up_b))
        back[...] = back_b + product(trans_b, turned_up)
        trans[...] = product(trans_b, down)
        up[...] = product(up_a, up_b) + product(bounce, turned_up)
        refl[...] = refl_a + product(bounce, down)

    solve(product(back_a, refl_b), use, power, total)


def times(left, right, out):
    out[...] = product(left[...], right[...])


def times_transpose(rows, matrix):
    return lax.dot_general(
        rows, matrix, (((1,), (1,)), ((), ())), precision=lax.Precision.HIGH, preferred_element_type=jnp.float32
    )


def last_step(odd, even, refl, field_out, bounced_out, field, bounced, sems):
    field[...] = jnp.where(lax.axis_index("depth") % 2 == 1, odd[...], even[...])
    rows = pltpu.make_async_copy(field, field_out, sems.at[0])
    rows.start()
    half = field.shape[0] // 2
    matrix_high, matrix_low = split(refl[...])
    dot = functools.partial(
        lax.dot_general, dimension_numbers=(((1,), (1,)), ((), ())), preferred_element_type=jnp.float32
    )
    copies = []
    for i in range(2):
        part = pl.ds(i * half, half)
        high, low = split(field[part, :])
        bounced[part, :] = dot(high, matrix_high) + (dot(high, matrix_low) + dot(low, matrix_high))
        copies.append(pltpu.make_async_copy(bounced.at[part, :], bounced_out.at[part, :], sems.at[1 + i]))
        copies[-1].start()
    rows.wait()
    for copy in copies:
        copy.wait()


def finish(odd, even, refl):
    shape = jax.ShapeDtypeStruct(odd.shape, jnp.float32)
    vmem, hbm = pl.BlockSpec(memory_space=pltpu.VMEM), pl.BlockSpec(memory_space=pl.ANY)
    return pl.pallas_call(
        last_step,
        out_shape=[shape, shape],
        in_specs=[vmem] * 3,
        out_specs=[hbm, hbm],
        scratch_shapes=[pltpu.VMEM(odd.shape, jnp.float32)] * 2 + [pltpu.SemaphoreType.DMA((3,))],
        compiler_params=pltpu.CompilerParams(vmem_limit_bytes=12 * 2**20),
    )(odd, even, refl)


def filled(useful, groups, count):
    def mate(device):
        return (device[0] ^ 1, device[1])

    pairs = dict(useful)
    targets = set(pairs.values())
    devices = [(g, s) for g in range(groups) for s in range(count)]
    for device in devices:
        if device not in pairs and mate(device) not in targets:
            pairs[device] = mate(device)
    spare = set(devices) - set(pairs.values())
    for source, target in useful.items():
        if mate(target) not in pairs and mate(source) in spare:
            pairs[mate(target)] = mate(source)
            spare.discard(mate(source))
    return pairs


def shards(slabs, incident):
    groups, count = lax.axis_size("depth"), lax.axis_size("slab")
    group, place = lax.axis_index("depth"), lax.axis_index("slab")
    levels = count.bit_length() - 1
    parity = group % 2
    pair, side = place // 2, place % 2
    pairs = count // 2

    def send(block, useful, fill=True):
        route = filled(useful, groups, count) if fill else useful
        route = sorted((a[0] * count + a[1], b[0] * count + b[1]) for a, b in route.items())
        return lax.ppermute(block, AXES, route)

    def turn(g, k):
        return g % 2 if k < pairs - 1 else 0

    def home(g, k):
        return (g, 2 * k + turn(g, k))

    def guest(g, k):
        return (g, 2 * k + 1 - turn(g, k))

    turned = jnp.where(pair == pairs - 1, 0, parity)
    owners = [list(range(pairs))]
    merges = []
    while len(owners[-1]) > 1:
        now, kept = owners[-1], []
        merges.append([])
        for k in range(0, len(now), 2):
            below = len(now) > 2 and k // 2 % 2 == 0
            merges[-1].append((now[k], now[k + 1], True) if below else (now[k + 1], now[k], False))
            kept.append(merges[-1][-1][1])
        owners.append(kept)

    def routes(level, late=False):
        return {
            home(g, source): home(g, target)
            for source, target, below in merges[level - 1]
            if below or not late
            for g in range(groups)
        }

    def is_one(some):
        return functools.reduce(jnp.logical_or, [pair == k for k in some], False)

    def marks(level):
        odd, at = lax.axis_index("depth") % 2, lax.axis_index("slab") // 2

        def among(some):
            return functools.reduce(jnp.maximum, [(at == k).astype(jnp.int32) for k in some], jnp.int32(0))

        below = among([m[1] for m in merges[max(level, 1) - 1] if m[2]])
        if level > 1:
            return jnp.int32(0), jnp.int32(0), below
        return (1 - among([pairs - 1])) * odd, among([m[1] for m in merges[0] if m[0] < pairs - 1]) * odd, below

    own = slabs[0, 0]
    injected = incident[0]
    spread = {guest(g, k): home(g, k) for g in range(groups) for k in range(pairs)}
    spread_late = {guest(g, k): home(g, k) for g in range(groups) for k in range(pairs - 1)}
    chosen = lax.dynamic_index_in_dim(own, 2 * turned, keepdims=False)
    chosen, after = lax.optimization_barrier((chosen, own))
    came = [send(chosen, spread), send(after[1], spread), send(after[3], spread_late)]
    came.append(send(lax.dynamic_index_in_dim(after, 2 - 2 * turned, keepdims=False), spread_late))
    first = functools.partial(marks, 1)
    split_level = levels - 2
    late = split_level == 1
    out0, down, solver, bounce = call(functools.partial(first_step, first), [own, came[0]], 4, True)
    sent = [send(out0, routes(1))]
    back, up = call(functools.partial(first_rest, first), [own, solver, bounce], 2)
    out1, kept = call(functools.partial(second_step, first), [down, back, up, came[1]], 2)
    sent.append(send(out1, routes(1)))
    out2, rest = call(functools.partial(third_step, first), [down, up, kept, came[2]], 2)
    sent.append(send(out2, routes(1, late)))
    out3 = came[3] + rest
    sent.append(send(out3, routes(1, late)))
    state = [out0, out1, out2, out3]
    for level in range(1, split_level):
        state = call(functools.partial(any_run, functools.partial(marks, level)), state + sent, 4, True)
        late = level + 1 == split_level
        sent = [send(block, routes(level + 1, late and i > 1)) for i, block in enumerate(state)]

    top = routes(levels - 1)
    split_marks = functools.partial(marks, split_level)
    low_refl, low_down = call(functools.partial(lower_run, split_marks), state + sent[:1], 2, True)
    low_refl = send(low_refl, top)
    (low_trans,) = call(times, [sent[1], low_down], 1)
    low_trans = send(low_trans, top)
    back_a, trans_a, solver = call(functools.partial(upper_run, split_marks), state + [sent[0], sent[1], sent[3]], 3, True)
    back_a, _ = lax.optimization_barrier((back_a, sent[2]))
    (down,) = call(whole_down, [back_a, trans_a, low_refl], 1, True)
    (trans,) = call(times, [low_trans, down], 1)
    (refl,) = call(functools.partial(whole_refl, split_marks), [state[0], state[2], state[3]] + sent + [solver, low_refl, down], 1)

    def line(g, k):
        return (g, 2 * k + g % 2)

    def hand_out(block, fill, order):
        level = levels - 1
        while level > 0:
            steps = []
            for far, near, _ in merges[level - 1]:
                if level > 1:
                    below = {m[1]: m[0] for m in merges[level - 2]}
                    steps.append([[(near, below[far]), (near, far), (near, below[near])][n] for n in order])
                else:
                    steps.append([(near, far)])
            got = block
            for step, full in zip(zip(*steps), fill):
                fresh = is_one([target for _, target in step])
                route = {line(g, a): line(g, b) for a, b in step for g in range(groups)}
                got = jnp.where(fresh, send(block, route, full), got)
            block = got
            level -= 2
        return block

    trans, _ = lax.optimization_barrier((hand_out(trans, (True, True, True), (1, 0, 2)), refl))
    refl = hand_out(refl, (False, False, False), (0, 1, 2))

    across = {}
    for g in range(groups):
        for k in range(pairs):
            across[line(g, k)] = (g | 1, 2 * k + 1 - g % 2)
    swap = {(g, s): (g ^ 1, s) for g in range(groups) for s in range(count)}
    crossed = send(trans, across, False)
    trans_even = jnp.where(side == 1, crossed, send(trans, swap))
    trans_odd = jnp.where(side == 1, trans, crossed)
    even = send(injected, swap)
    opposite = {line(g, k): (g, line(g, k)[1] ^ 1) for g in range(groups) for k in range(pairs)}
    spread_refl = jnp.where(side == parity, refl, send(refl, opposite))
    handed = jnp.zeros_like(injected)
    for j in range(0, groups, 2):
        field_even = even + handed
        field_odd = injected + times_transpose(field_even, trans_even)
        if j + 2 < groups:
            leaving, _ = lax.optimization_barrier((times_transpose(field_odd, trans_odd), refl))
            arriving = send(leaving, {(j + 1, s): (j + 3, s) for s in range(count)})
            arriving, _ = lax.optimization_barrier((arriving, spread_refl))
            handed = jnp.where(group // 2 == j // 2 + 1, arriving, handed)
    field, bounced = finish(field_odd, send(field_even, swap), spread_refl)
    return (field[None], bounced[None])


def solution(mesh):
    placed = (P("depth", "slab", None, None, None), P("depth", "slab", None))
    return jax.shard_map(
        shards,
        mesh=mesh,
        in_specs=placed,
        out_specs=(P("depth", "slab", None), P("depth", "slab", None)),
        check_vma=False,
    )
```

```python
import functools

import jax
import jax.numpy as jnp
from jax import lax
from jax.experimental import pallas as pl
from jax.experimental.pallas import tpu as pltpu
from jax.sharding import PartitionSpec as P

AXES = ("depth", "slab")


def split(value):
    high = value.astype(jnp.bfloat16)
    return high, (value - high.astype(jnp.float32)).astype(jnp.bfloat16)


def product(left, right):
    left_high, left_low = split(left)
    right_high, right_low = split(right)
    dot = functools.partial(jnp.dot, preferred_element_type=jnp.float32)
    return dot(left_high, right_high) + (dot(left_high, right_low) + dot(left_low, right_high))


def rough(left, right):
    return jnp.dot(left.astype(jnp.bfloat16), right.astype(jnp.bfloat16), preferred_element_type=jnp.float32)


def solve(coupling, use, power, total):
    order = coupling.shape[0]
    row = lax.broadcasted_iota(jnp.int32, (order, order), 0)
    column = lax.broadcasted_iota(jnp.int32, (order, order), 1)
    start = coupling + jnp.where(row == column, 1.0, 0.0)
    squared = product(coupling, coupling)
    power[...] = squared
    total[...] = start
    size = jnp.sum(squared * squared)
    result = start + (squared + rough(coupling, squared))
    use(result + rough(rough(squared, squared), result))

    @pl.when(size > 2.0**-10)
    def _():
        total[...] += product(total[...], power[...])

        def more(state):
            turn, last = state
            return jnp.logical_and(turn < 40, last > 2.0**-24)

        def step(state):
            turn, _ = state
            following = product(power[...], power[...])
            total[...] += product(total[...], following)
            power[...] = following
            return turn + 1, jnp.sum(following * following)

        lax.while_loop(more, step, (0, size))
        use(total[...])


def call(body, blocks, outs, solves=False):
    order = blocks[0].shape[-1]
    square = jax.ShapeDtypeStruct((order, order), jnp.float32)
    vmem = pl.BlockSpec(memory_space=pltpu.VMEM)
    results = pl.pallas_call(
        body,
        out_shape=[square] * outs,
        in_specs=[vmem] * len(blocks),
        out_specs=[vmem] * outs,
        scratch_shapes=[pltpu.VMEM((order, order), jnp.float32)] * 2 if solves else [],
        compiler_params=pltpu.CompilerParams(vmem_limit_bytes=12 * 2**20),
    )(*blocks)
    return list(results)


def first_step(marks, refl, trans, up, behind, c0, out0, down, solver, bounce, power, total):
    turned = marks()[0] == 1
    bounce[...] = product(jnp.where(turned, trans[...], up[...]), c0[...])

    def use(value):
        solver[...] = value
        down[...] = product(value, jnp.where(turned, up[...], trans[...]))
        out0[...] = refl[...] + product(bounce[...], down[...])

    solve(product(behind[...], c0[...]), use, power, total)


def first_rest(marks, trans, up, behind, solver, bounce, back, upward):
    turned = marks()[0] == 1
    back[...] = product(solver[...], behind[...])
    upward[...] = jnp.where(turned, trans[...], up[...]) + product(bounce[...], back[...])


def pick(marks, which, own, *rest):
    outs, sems = rest[:-1], rest[-1]
    turned = 2 * marks()[0]
    places = (turned, 1, 3, 2 - turned)
    copies = [pltpu.make_async_copy(own.at[places[i]], out, sems.at[n]) for n, (i, out) in enumerate(zip(which, outs))]
    for copy in copies:
        copy.start()
    for copy in copies:
        copy.wait()


def picked(marks, which, own):
    block = jax.ShapeDtypeStruct(own.shape[1:], jnp.float32)
    vmem = pl.BlockSpec(memory_space=pltpu.VMEM)
    return list(pl.pallas_call(
        functools.partial(pick, marks, which),
        out_shape=[block] * len(which),
        in_specs=[pl.BlockSpec(memory_space=pltpu.HBM)],
        out_specs=[vmem] * len(which),
        scratch_shapes=[pltpu.SemaphoreType.DMA((len(which),))],
        compiler_params=pltpu.CompilerParams(vmem_limit_bytes=12 * 2**20),
    )(pltpu.with_memory_space_constraint(own, pltpu.HBM)))


def second_step(marks, down, back, up, c1, out1, kept):
    turned = marks()[0] == 1
    out1[...] = product(jnp.where(turned, up[...], c1[...]), jnp.where(turned, c1[...], down[...]))
    kept[...] = product(jnp.where(turned, back[...], c1[...]), jnp.where(turned, c1[...], back[...]))


def third_step(marks, down, up, kept, c2, out2, rest):
    turned = marks()[0] == 1
    out2[...] = product(jnp.where(turned, c2[...], up[...]), jnp.where(turned, down[...], c2[...]))
    rest[...] = product(jnp.where(turned, c2[...], kept[...]), jnp.where(turned, kept[...], c2[...]))


def ordered(turned, first, last):
    return jnp.where(turned, last[...], first[...]), jnp.where(turned, first[...], last[...])


def lower_run(marks, o0, o1, o2, o3, refl_b, refl, down, power, total):
    refl_a, back_a = ordered(marks()[0] == 1, o0, o3)
    bounce = product(o2[...], refl_b[...])

    def use(value):
        down[...] = product(value, o1[...])
        refl[...] = refl_a + product(bounce, down[...])

    solve(product(back_a, refl_b[...]), use, power, total)


def upper_run(marks, o0, o1, o2, o3, c0, c1, c3, back, trans, solver, power, total):
    mark = marks()
    refl_b, back_b = ordered(mark[0] == 1, o0, o3)
    _, back_a = ordered(mark[1] == 1, c0, c3)
    turned_up = product(back_a, o2[...])

    def use(value):
        solver[...] = value
        through = product(o1[...], value)
        back[...] = back_b + product(through, turned_up)
        trans[...] = product(through, c1[...])

    solve(product(back_a, refl_b), use, power, total)


def whole_down(back_a, trans_a, refl_b, down, power, total):
    def use(value):
        down[...] = product(value, trans_a[...])

    solve(product(back_a[...], refl_b[...]), use, power, total)


def whole_refl(marks, o0, o2, o3, c0, c1, c2, c3, solver, low_refl, down, refl):
    mark = marks()
    refl_b, _ = ordered(mark[0] == 1, o0, o3)
    refl_a, back_a = ordered(mark[1] == 1, c0, c3)
    first = refl_a + product(c2[...], product(refl_b, product(solver[...], c1[...])))
    turned_up = product(solver[...], product(back_a, o2[...]))
    up = product(c2[...], o2[...] + product(refl_b, turned_up))
    refl[...] = first + product(up, product(low_refl[...], down[...]))


def any_run(marks, o0, o1, o2, o3, c0, c1, c2, c3, refl, trans, up, back, power, total):
    mark = marks()
    refl_own, back_own = ordered(mark[0] == 1, o0, o3)
    refl_came, back_came = ordered(mark[1] == 1, c0, c3)
    own, came = (refl_own, o1[...], o2[...], back_own), (refl_came, c1[...], c2[...], back_came)
    below = mark[2] == 1
    refl_a, trans_a, up_a, back_a = [jnp.where(below, c, o) for o, c in zip(own, came)]
    refl_b, trans_b, up_b, back_b = [jnp.where(below, o, c) for o, c in zip(own, came)]
    bounce = product(up_a, refl_b)

    def use(value):
        down = product(value, trans_a)
        turned_up = product(value, product(back_a, up_b))
        back[...] = back_b + product(trans_b, turned_up)
        trans[...] = product(trans_b, down)
        up[...] = product(up_a, up_b) + product(bounce, turned_up)
        refl[...] = refl_a + product(bounce, down)

    solve(product(back_a, refl_b), use, power, total)


def times(left, right, out):
    out[...] = product(left[...], right[...])


def times_transpose(rows, matrix):
    return lax.dot_general(
        rows, matrix, (((1,), (1,)), ((), ())), precision=lax.Precision.HIGH, preferred_element_type=jnp.float32
    )


def last_step(odd, even, refl, field_out, bounced_out, field, bounced, sems):
    field[...] = jnp.where(lax.axis_index("depth") % 2 == 1, odd[...], even[...])
    rows = pltpu.make_async_copy(field, field_out, sems.at[0])
    rows.start()
    half = field.shape[0] // 2
    matrix_high, matrix_low = split(refl[...])
    dot = functools.partial(
        lax.dot_general, dimension_numbers=(((1,), (1,)), ((), ())), preferred_element_type=jnp.float32
    )
    copies = []
    for i in range(2):
        part = pl.ds(i * half, half)
        high, low = split(field[part, :])
        bounced[part, :] = dot(high, matrix_high) + (dot(high, matrix_low) + dot(low, matrix_high))
        copies.append(pltpu.make_async_copy(bounced.at[part, :], bounced_out.at[part, :], sems.at[1 + i]))
        copies[-1].start()
    rows.wait()
    for copy in copies:
        copy.wait()


def finish(odd, even, refl):
    shape = jax.ShapeDtypeStruct(odd.shape, jnp.float32)
    vmem, hbm = pl.BlockSpec(memory_space=pltpu.VMEM), pl.BlockSpec(memory_space=pl.ANY)
    return pl.pallas_call(
        last_step,
        out_shape=[shape, shape],
        in_specs=[vmem] * 3,
        out_specs=[hbm, hbm],
        scratch_shapes=[pltpu.VMEM(odd.shape, jnp.float32)] * 2 + [pltpu.SemaphoreType.DMA((3,))],
        compiler_params=pltpu.CompilerParams(vmem_limit_bytes=12 * 2**20),
    )(odd, even, refl)


def filled(useful, groups, count):
    def mate(device):
        return (device[0] ^ 1, device[1])

    pairs = dict(useful)
    targets = set(pairs.values())
    devices = [(g, s) for g in range(groups) for s in range(count)]
    for device in devices:
        if device not in pairs and mate(device) not in targets:
            pairs[device] = mate(device)
    spare = set(devices) - set(pairs.values())
    for source, target in useful.items():
        if mate(target) not in pairs and mate(source) in spare:
            pairs[mate(target)] = mate(source)
            spare.discard(mate(source))
    return pairs


def shards(slabs, incident):
    groups, count = lax.axis_size("depth"), lax.axis_size("slab")
    group, place = lax.axis_index("depth"), lax.axis_index("slab")
    levels = count.bit_length() - 1
    parity = group % 2
    pair, side = place // 2, place % 2
    pairs = count // 2

    def send(block, useful, fill=True):
        route = filled(useful, groups, count) if fill else useful
        route = sorted((a[0] * count + a[1], b[0] * count + b[1]) for a, b in route.items())
        return lax.ppermute(block, AXES, route)

    def turn(g, k):
        return g % 2 if k < pairs - 1 else 0

    def home(g, k):
        return (g, 2 * k + turn(g, k))

    def guest(g, k):
        return (g, 2 * k + 1 - turn(g, k))

    turned = jnp.where(pair == pairs - 1, 0, parity)
    owners = [list(range(pairs))]
    merges = []
    while len(owners[-1]) > 1:
        now, kept = owners[-1], []
        merges.append([])
        for k in range(0, len(now), 2):
            below = len(now) > 2 and k // 2 % 2 == 0
            merges[-1].append((now[k], now[k + 1], True) if below else (now[k + 1], now[k], False))
            kept.append(merges[-1][-1][1])
        owners.append(kept)

    def routes(level, late=False):
        return {
            home(g, source): home(g, target)
            for source, target, below in merges[level - 1]
            if below or not late
            for g in range(groups)
        }

    def is_one(some):
        return functools.reduce(jnp.logical_or, [pair == k for k in some], False)

    def marks(level):
        odd, at = lax.axis_index("depth") % 2, lax.axis_index("slab") // 2

        def among(some):
            return functools.reduce(jnp.maximum, [(at == k).astype(jnp.int32) for k in some], jnp.int32(0))

        below = among([m[1] for m in merges[max(level, 1) - 1] if m[2]])
        if level > 1:
            return jnp.int32(0), jnp.int32(0), below
        return (1 - among([pairs - 1])) * odd, among([m[1] for m in merges[0] if m[0] < pairs - 1]) * odd, below

    own = slabs[0, 0]
    injected = incident[0]
    spread = {guest(g, k): home(g, k) for g in range(groups) for k in range(pairs)}
    spread_late = {guest(g, k): home(g, k) for g in range(groups) for k in range(pairs - 1)}
    first = functools.partial(marks, 1)
    mine = picked(first, (0,), own)
    later, _ = lax.optimization_barrier((own, mine[0]))
    mine += picked(first, (1, 2, 3), later)
    came = [send(block, spread if n < 2 else spread_late) for n, block in enumerate(mine)]
    split_level = levels - 2
    late = split_level == 1
    out0, down, solver, bounce = call(functools.partial(first_step, first), mine + came[:1], 4, True)
    sent = [send(out0, routes(1))]
    back, up = call(functools.partial(first_rest, first), mine[1:] + [solver, bounce], 2)
    out1, kept = call(functools.partial(second_step, first), [down, back, up, came[1]], 2)
    sent.append(send(out1, routes(1)))
    out2, rest = call(functools.partial(third_step, first), [down, up, kept, came[2]], 2)
    sent.append(send(out2, routes(1, late)))
    out3 = came[3] + rest
    sent.append(send(out3, routes(1, late)))
    state = [out0, out1, out2, out3]
    for level in range(1, split_level):
        state = call(functools.partial(any_run, functools.partial(marks, level)), state + sent, 4, True)
        late = level + 1 == split_level
        sent = [send(block, routes(level + 1, late and i > 1)) for i, block in enumerate(state)]

    top = routes(levels - 1)
    split_marks = functools.partial(marks, split_level)
    low_refl, low_down = call(functools.partial(lower_run, split_marks), state + sent[:1], 2, True)
    low_refl = send(low_refl, top)
    (low_trans,) = call(times, [sent[1], low_down], 1)
    low_trans = send(low_trans, top)
    back_a, trans_a, solver = call(functools.partial(upper_run, split_marks), state + [sent[0], sent[1], sent[3]], 3, True)
    back_a, _ = lax.optimization_barrier((back_a, sent[2]))
    (down,) = call(whole_down, [back_a, trans_a, low_refl], 1, True)
    (trans,) = call(times, [low_trans, down], 1)
    (refl,) = call(functools.partial(whole_refl, split_marks), [state[0], state[2], state[3]] + sent + [solver, low_refl, down], 1)

    def line(g, k):
        return (g, 2 * k + g % 2)

    def hand_out(block, fill, order, last=0):
        level = levels - 1
        while level > 0:
            steps = []
            for far, near, _ in merges[level - 1]:
                if level > 1:
                    below = {m[1]: m[0] for m in merges[level - 2]}
                    steps.append([[(near, below[far]), (near, far), (near, below[near])][n] for n in order])
                else:
                    steps.append([(near, far)])
            got = block
            for step, full in zip(zip(*steps), fill):
                fresh = is_one([target for _, target in step])
                route = {line(g, a): line(g, b) for a, b in step for g in range(groups - last)}
                got = jnp.where(fresh, send(block, route, full), got)
            block = got
            level -= 2
        return block

    trans, _ = lax.optimization_barrier((hand_out(trans, (True, True, True), (1, 0, 2), 1), refl))
    refl = hand_out(refl, (False, False, False), (0, 1, 2))

    across = {}
    for g in range(groups - 1):
        for k in range(pairs):
            across[line(g, k)] = (g | 1, 2 * k + 1 - g % 2)
    swap = {(g, s): (g ^ 1, s) for g in range(groups) for s in range(count)}
    crossed = send(trans, across, False)
    trans_even = jnp.where(side == 1, crossed, send(trans, swap))
    trans_odd = jnp.where(side == 1, trans, crossed)
    even = send(injected, swap)
    opposite = {line(g, k): (g, line(g, k)[1] ^ 1) for g in range(groups) for k in range(pairs)}
    spread_refl = jnp.where(side == parity, refl, send(refl, opposite))
    handed = jnp.zeros_like(injected)
    for j in range(0, groups, 2):
        field_even = even + handed
        field_odd = injected + times_transpose(field_even, trans_even)
        if j + 2 < groups:
            leaving, _ = lax.optimization_barrier((times_transpose(field_odd, trans_odd), refl))
            arriving = send(leaving, {(j + 1, s): (j + 3, s) for s in range(count)})
            arriving, _ = lax.optimization_barrier((arriving, spread_refl))
            handed = jnp.where(group // 2 == j // 2 + 1, arriving, handed)
    field, bounced = finish(field_odd, send(field_even, swap), spread_refl)
    return (field[None], bounced[None])


def solution(mesh):
    placed = (P("depth", "slab", None, None, None), P("depth", "slab", None))
    return jax.shard_map(
        shards,
        mesh=mesh,
        in_specs=placed,
        out_specs=(P("depth", "slab", None), P("depth", "slab", None)),
        check_vma=False,
    )
```

```python
import functools

import jax
import jax.numpy as jnp
from jax import lax
from jax.experimental import pallas as pl
from jax.experimental.pallas import tpu as pltpu
from jax.sharding import PartitionSpec as P

AXES = ("depth", "slab")


def split(value):
    high = value.astype(jnp.bfloat16)
    return high, (value - high.astype(jnp.float32)).astype(jnp.bfloat16)


def product(left, right):
    left_high, left_low = split(left)
    right_high, right_low = split(right)
    dot = functools.partial(jnp.dot, preferred_element_type=jnp.float32)
    return dot(left_high, right_high) + (dot(left_high, right_low) + dot(left_low, right_high))


def rough(left, right):
    return jnp.dot(left.astype(jnp.bfloat16), right.astype(jnp.bfloat16), preferred_element_type=jnp.float32)


def solve(coupling, use, power, total):
    order = coupling.shape[0]
    row = lax.broadcasted_iota(jnp.int32, (order, order), 0)
    column = lax.broadcasted_iota(jnp.int32, (order, order), 1)
    start = coupling + jnp.where(row == column, 1.0, 0.0)
    squared = product(coupling, coupling)
    power[...] = squared
    total[...] = start
    size = jnp.sum(squared * squared)
    result = start + (squared + rough(coupling, squared))
    use(result + rough(rough(squared, squared), result))

    @pl.when(size > 2.0**-10)
    def _():
        total[...] += product(total[...], power[...])

        def more(state):
            turn, last = state
            return jnp.logical_and(turn < 40, last > 2.0**-24)

        def step(state):
            turn, _ = state
            following = product(power[...], power[...])
            total[...] += product(total[...], following)
            power[...] = following
            return turn + 1, jnp.sum(following * following)

        lax.while_loop(more, step, (0, size))
        use(total[...])


def call(body, blocks, outs, solves=False):
    order = blocks[0].shape[-1]
    square = jax.ShapeDtypeStruct((order, order), jnp.float32)
    vmem = pl.BlockSpec(memory_space=pltpu.VMEM)
    results = pl.pallas_call(
        body,
        out_shape=[square] * outs,
        in_specs=[vmem] * len(blocks),
        out_specs=[vmem] * outs,
        scratch_shapes=[pltpu.VMEM((order, order), jnp.float32)] * 2 if solves else [],
        compiler_params=pltpu.CompilerParams(vmem_limit_bytes=12 * 2**20),
    )(*blocks)
    return list(results)


def first_step(marks, refl, trans, up, behind, c0, out0, down, solver, bounce, power, total):
    turned = marks()[0] == 1
    bounce[...] = product(jnp.where(turned, trans[...], up[...]), c0[...])

    def use(value):
        solver[...] = value
        down[...] = product(value, jnp.where(turned, up[...], trans[...]))
        out0[...] = refl[...] + product(bounce[...], down[...])

    solve(product(behind[...], c0[...]), use, power, total)


def first_rest(marks, trans, up, behind, solver, bounce, back, upward):
    turned = marks()[0] == 1
    back[...] = product(solver[...], behind[...])
    upward[...] = jnp.where(turned, trans[...], up[...]) + product(bounce[...], back[...])


def pick(marks, which, own, *rest):
    outs, sems = rest[:-1], rest[-1]
    turned = 2 * marks()[0]
    places = (turned, 1, 3, 2 - turned)
    copies = [pltpu.make_async_copy(own.at[places[i]], out, sems.at[n]) for n, (i, out) in enumerate(zip(which, outs))]
    for copy in copies:
        copy.start()
    for copy in copies:
        copy.wait()


def picked(marks, which, own):
    block = jax.ShapeDtypeStruct(own.shape[1:], jnp.float32)
    vmem = pl.BlockSpec(memory_space=pltpu.VMEM)
    return list(pl.pallas_call(
        functools.partial(pick, marks, which),
        out_shape=[block] * len(which),
        in_specs=[pl.BlockSpec(memory_space=pltpu.HBM)],
        out_specs=[vmem] * len(which),
        scratch_shapes=[pltpu.SemaphoreType.DMA((len(which),))],
        compiler_params=pltpu.CompilerParams(vmem_limit_bytes=12 * 2**20),
    )(pltpu.with_memory_space_constraint(own, pltpu.HBM)))


def second_step(marks, down, back, up, c1, out1, kept):
    turned = marks()[0] == 1
    out1[...] = product(jnp.where(turned, up[...], c1[...]), jnp.where(turned, c1[...], down[...]))
    kept[...] = product(jnp.where(turned, back[...], c1[...]), jnp.where(turned, c1[...], back[...]))


def third_step(marks, down, up, kept, c2, out2, rest):
    turned = marks()[0] == 1
    out2[...] = product(jnp.where(turned, c2[...], up[...]), jnp.where(turned, down[...], c2[...]))
    rest[...] = product(jnp.where(turned, c2[...], kept[...]), jnp.where(turned, kept[...], c2[...]))


def ordered(turned, first, last):
    return jnp.where(turned, last[...], first[...]), jnp.where(turned, first[...], last[...])


def lower_run(marks, o0, o1, o2, o3, refl_b, refl, down, power, total):
    refl_a, back_a = ordered(marks()[0] == 1, o0, o3)
    bounce = product(o2[...], refl_b[...])

    def use(value):
        down[...] = product(value, o1[...])
        refl[...] = refl_a + product(bounce, down[...])

    solve(product(back_a, refl_b[...]), use, power, total)


def upper_run(marks, o0, o1, o2, o3, c0, c1, c3, back, trans, solver, power, total):
    mark = marks()
    refl_b, back_b = ordered(mark[0] == 1, o0, o3)
    _, back_a = ordered(mark[1] == 1, c0, c3)
    turned_up = product(back_a, o2[...])

    def use(value):
        solver[...] = value
        through = product(o1[...], value)
        back[...] = back_b + product(through, turned_up)
        trans[...] = product(through, c1[...])

    solve(product(back_a, refl_b), use, power, total)


def whole_down(back_a, trans_a, refl_b, down, power, total):
    def use(value):
        down[...] = product(value, trans_a[...])

    solve(product(back_a[...], refl_b[...]), use, power, total)


def whole_refl(marks, o0, o2, o3, c0, c1, c2, c3, solver, low_refl, down, refl):
    mark = marks()
    refl_b, _ = ordered(mark[0] == 1, o0, o3)
    refl_a, back_a = ordered(mark[1] == 1, c0, c3)
    first = refl_a + product(c2[...], product(refl_b, product(solver[...], c1[...])))
    turned_up = product(solver[...], product(back_a, o2[...]))
    up = product(c2[...], o2[...] + product(refl_b, turned_up))
    refl[...] = first + product(up, product(low_refl[...], down[...]))


def any_run(marks, o0, o1, o2, o3, c0, c1, c2, c3, refl, trans, up, back, power, total):
    mark = marks()
    refl_own, back_own = ordered(mark[0] == 1, o0, o3)
    refl_came, back_came = ordered(mark[1] == 1, c0, c3)
    own, came = (refl_own, o1[...], o2[...], back_own), (refl_came, c1[...], c2[...], back_came)
    below = mark[2] == 1
    refl_a, trans_a, up_a, back_a = [jnp.where(below, c, o) for o, c in zip(own, came)]
    refl_b, trans_b, up_b, back_b = [jnp.where(below, o, c) for o, c in zip(own, came)]
    bounce = product(up_a, refl_b)

    def use(value):
        down = product(value, trans_a)
        turned_up = product(value, product(back_a, up_b))
        back[...] = back_b + product(trans_b, turned_up)
        trans[...] = product(trans_b, down)
        up[...] = product(up_a, up_b) + product(bounce, turned_up)
        refl[...] = refl_a + product(bounce, down)

    solve(product(back_a, refl_b), use, power, total)


def times(left, right, out):
    out[...] = product(left[...], right[...])


def times_transpose(rows, matrix):
    return lax.dot_general(
        rows, matrix, (((1,), (1,)), ((), ())), precision=lax.Precision.HIGH, preferred_element_type=jnp.float32
    )


def rows_times(rows, matrix):
    rows_high, rows_low = split(rows)
    high, low = split(matrix)
    dot = functools.partial(
        lax.dot_general, dimension_numbers=(((1,), (1,)), ((), ())), preferred_element_type=jnp.float32
    )
    return dot(rows_high, high) + (dot(rows_high, low) + dot(rows_low, high))


def sweep_odd(even, injected, trans, crossed, swapped, field):
    lower_side = lax.axis_index("slab") % 2 == 1
    field[...] = injected[...] + rows_times(even[...], jnp.where(lower_side, crossed[...], swapped[...]))


def sweep_on(even, injected, trans, crossed, swapped, leaving):
    lower_side = lax.axis_index("slab") % 2 == 1
    field = injected[...] + rows_times(even[...], jnp.where(lower_side, crossed[...], swapped[...]))
    leaving[...] = rows_times(field, jnp.where(lower_side, trans[...], crossed[...]))


def last_step(odd, even, refl, field_out, bounced_out, field, bounced, sems):
    field[...] = jnp.where(lax.axis_index("depth") % 2 == 1, odd[...], even[...])
    rows = pltpu.make_async_copy(field, field_out, sems.at[0])
    rows.start()
    half = field.shape[0] // 2
    matrix_high, matrix_low = split(refl[...])
    dot = functools.partial(
        lax.dot_general, dimension_numbers=(((1,), (1,)), ((), ())), preferred_element_type=jnp.float32
    )
    copies = []
    for i in range(2):
        part = pl.ds(i * half, half)
        high, low = split(field[part, :])
        bounced[part, :] = dot(high, matrix_high) + (dot(high, matrix_low) + dot(low, matrix_high))
        copies.append(pltpu.make_async_copy(bounced.at[part, :], bounced_out.at[part, :], sems.at[1 + i]))
        copies[-1].start()
    rows.wait()
    for copy in copies:
        copy.wait()


def finish(odd, even, refl):
    shape = jax.ShapeDtypeStruct(odd.shape, jnp.float32)
    vmem, hbm = pl.BlockSpec(memory_space=pltpu.VMEM), pl.BlockSpec(memory_space=pl.ANY)
    return pl.pallas_call(
        last_step,
        out_shape=[shape, shape],
        in_specs=[vmem] * 3,
        out_specs=[hbm, hbm],
        scratch_shapes=[pltpu.VMEM(odd.shape, jnp.float32)] * 2 + [pltpu.SemaphoreType.DMA((3,))],
        compiler_params=pltpu.CompilerParams(vmem_limit_bytes=12 * 2**20),
    )(odd, even, refl)


def filled(useful, groups, count):
    def mate(device):
        return (device[0] ^ 1, device[1])

    pairs = dict(useful)
    targets = set(pairs.values())
    devices = [(g, s) for g in range(groups) for s in range(count)]
    for device in devices:
        if device not in pairs and mate(device) not in targets:
            pairs[device] = mate(device)
    spare = set(devices) - set(pairs.values())
    for source, target in useful.items():
        if mate(target) not in pairs and mate(source) in spare:
            pairs[mate(target)] = mate(source)
            spare.discard(mate(source))
    return pairs


def shards(slabs, incident):
    groups, count = lax.axis_size("depth"), lax.axis_size("slab")
    group, place = lax.axis_index("depth"), lax.axis_index("slab")
    levels = count.bit_length() - 1
    parity = group % 2
    pair, side = place // 2, place % 2
    pairs = count // 2

    def send(block, useful, fill=True):
        route = filled(useful, groups, count) if fill else useful
        route = sorted((a[0] * count + a[1], b[0] * count + b[1]) for a, b in route.items())
        return lax.ppermute(block, AXES, route)

    def turn(g, k):
        return g % 2 if k < pairs - 1 else 0

    def home(g, k):
        return (g, 2 * k + turn(g, k))

    def guest(g, k):
        return (g, 2 * k + 1 - turn(g, k))

    turned = jnp.where(pair == pairs - 1, 0, parity)
    owners = [list(range(pairs))]
    merges = []
    while len(owners[-1]) > 1:
        now, kept = owners[-1], []
        merges.append([])
        for k in range(0, len(now), 2):
            below = len(now) > 2 and k // 2 % 2 == 0
            merges[-1].append((now[k], now[k + 1], True) if below else (now[k + 1], now[k], False))
            kept.append(merges[-1][-1][1])
        owners.append(kept)

    def routes(level, late=False):
        return {
            home(g, source): home(g, target)
            for source, target, below in merges[level - 1]
            if below or not late
            for g in range(groups)
        }

    def is_one(some):
        return functools.reduce(jnp.logical_or, [pair == k for k in some], False)

    def marks(level):
        odd, at = lax.axis_index("depth") % 2, lax.axis_index("slab") // 2

        def among(some):
            return functools.reduce(jnp.maximum, [(at == k).astype(jnp.int32) for k in some], jnp.int32(0))

        below = among([m[1] for m in merges[max(level, 1) - 1] if m[2]])
        if level > 1:
            return jnp.int32(0), jnp.int32(0), below
        return (1 - among([pairs - 1])) * odd, among([m[1] for m in merges[0] if m[0] < pairs - 1]) * odd, below

    own = slabs[0, 0]
    injected = incident[0]
    spread = {guest(g, k): home(g, k) for g in range(groups) for k in range(pairs)}
    spread_late = {guest(g, k): home(g, k) for g in range(groups) for k in range(pairs - 1)}
    first = functools.partial(marks, 1)
    mine = picked(first, (0,), own)
    later, _ = lax.optimization_barrier((own, mine[0]))
    mine += picked(first, (1, 2, 3), later)
    came = [send(block, spread if n < 2 else spread_late) for n, block in enumerate(mine)]
    split_level = levels - 2
    late = split_level == 1
    out0, down, solver, bounce = call(functools.partial(first_step, first), mine + came[:1], 4, True)
    sent = [send(out0, routes(1))]
    back, up = call(functools.partial(first_rest, first), mine[1:] + [solver, bounce], 2)
    out1, kept = call(functools.partial(second_step, first), [down, back, up, came[1]], 2)
    sent.append(send(out1, routes(1)))
    out2, rest = call(functools.partial(third_step, first), [down, up, kept, came[2]], 2)
    sent.append(send(out2, routes(1, late)))
    out3 = came[3] + rest
    sent.append(send(out3, routes(1, late)))
    state = [out0, out1, out2, out3]
    for level in range(1, split_level):
        state = call(functools.partial(any_run, functools.partial(marks, level)), state + sent, 4, True)
        late = level + 1 == split_level
        sent = [send(block, routes(level + 1, late and i > 1)) for i, block in enumerate(state)]

    top = routes(levels - 1)
    split_marks = functools.partial(marks, split_level)
    low_refl, low_down = call(functools.partial(lower_run, split_marks), state + sent[:1], 2, True)
    low_refl = send(low_refl, top)
    (low_trans,) = call(times, [sent[1], low_down], 1)
    low_trans = send(low_trans, top)
    back_a, trans_a, solver = call(functools.partial(upper_run, split_marks), state + [sent[0], sent[1], sent[3]], 3, True)
    back_a, _ = lax.optimization_barrier((back_a, sent[2]))
    (down,) = call(whole_down, [back_a, trans_a, low_refl], 1, True)
    (trans,) = call(times, [low_trans, down], 1)
    (refl,) = call(functools.partial(whole_refl, split_marks), [state[0], state[2], state[3]] + sent + [solver, low_refl, down], 1)

    def line(g, k):
        return (g, 2 * k + g % 2)

    def hand_out(block, fill, order, last=0):
        level = levels - 1
        while level > 0:
            steps = []
            for far, near, _ in merges[level - 1]:
                if level > 1:
                    below = {m[1]: m[0] for m in merges[level - 2]}
                    steps.append([[(near, below[far]), (near, far), (near, below[near])][n] for n in order])
                else:
                    steps.append([(near, far)])
            got = block
            for step, full in zip(zip(*steps), fill):
                fresh = is_one([target for _, target in step])
                route = {line(g, a): line(g, b) for a, b in step for g in range(groups - last)}
                got = jnp.where(fresh, send(block, route, full), got)
            block = got
            level -= 2
        return block

    trans, _ = lax.optimization_barrier((hand_out(trans, (True, True, True), (1, 0, 2), 1), refl))
    refl = hand_out(refl, (False, False, False), (0, 1, 2))

    across = {}
    for g in range(groups - 1):
        for k in range(pairs):
            across[line(g, k)] = (g | 1, 2 * k + 1 - g % 2)
    swap = {(g, s): (g ^ 1, s) for g in range(groups) for s in range(count)}
    crossed = send(trans, across, False)
    swapped = send(trans, swap)
    even = send(injected, swap)
    opposite = {line(g, k): (g, line(g, k)[1] ^ 1) for g in range(groups) for k in range(pairs)}
    spread_refl = jnp.where(side == parity, refl, send(refl, opposite))
    handed = jnp.zeros_like(injected)
    for j in range(0, groups, 2):
        field_even = even + handed
        known = [field_even, injected, trans, crossed, swapped]
        if j + 2 < groups:
            (leaving,) = call(sweep_on, known, 1)
            leaving, _ = lax.optimization_barrier((leaving, refl))
            arriving = send(leaving, {(j + 1, s): (j + 3, s) for s in range(count)})
            arriving, _ = lax.optimization_barrier((arriving, spread_refl))
            handed = jnp.where(group // 2 == j // 2 + 1, arriving, handed)
    (field_odd,) = call(sweep_odd, known, 1)
    field, bounced = finish(field_odd, send(field_even, swap), spread_refl)
    return (field[None], bounced[None])


def solution(mesh):
    placed = (P("depth", "slab", None, None, None), P("depth", "slab", None))
    return jax.shard_map(
        shards,
        mesh=mesh,
        in_specs=placed,
        out_specs=(P("depth", "slab", None), P("depth", "slab", None)),
        check_vma=False,
    )
```

```python
import functools

import jax
import jax.numpy as jnp
from jax import lax
from jax.experimental import pallas as pl
from jax.experimental.pallas import tpu as pltpu
from jax.sharding import PartitionSpec as P

AXES = ("depth", "slab")


def split(value):
    high = value.astype(jnp.bfloat16)
    return high, (value - high.astype(jnp.float32)).astype(jnp.bfloat16)


def product(left, right):
    left_high, left_low = split(left)
    right_high, right_low = split(right)
    dot = functools.partial(jnp.dot, preferred_element_type=jnp.float32)
    return dot(left_high, right_high) + (dot(left_high, right_low) + dot(left_low, right_high))


def rough(left, right):
    return jnp.dot(left.astype(jnp.bfloat16), right.astype(jnp.bfloat16), preferred_element_type=jnp.float32)


def solve(coupling, use, power, total):
    order = coupling.shape[0]
    row = lax.broadcasted_iota(jnp.int32, (order, order), 0)
    column = lax.broadcasted_iota(jnp.int32, (order, order), 1)
    start = coupling + jnp.where(row == column, 1.0, 0.0)
    squared = product(coupling, coupling)
    power[...] = squared
    total[...] = start
    size = jnp.sum(squared * squared)
    result = start + (squared + rough(coupling, squared))
    use(result + rough(rough(squared, squared), result))

    @pl.when(size > 2.0**-10)
    def _():
        total[...] += product(total[...], power[...])

        def more(state):
            turn, last = state
            return jnp.logical_and(turn < 40, last > 2.0**-24)

        def step(state):
            turn, _ = state
            following = product(power[...], power[...])
            total[...] += product(total[...], following)
            power[...] = following
            return turn + 1, jnp.sum(following * following)

        lax.while_loop(more, step, (0, size))
        use(total[...])


def call(body, blocks, outs, solves=False):
    order = blocks[0].shape[-1]
    square = jax.ShapeDtypeStruct((order, order), jnp.float32)
    vmem = pl.BlockSpec(memory_space=pltpu.VMEM)
    results = pl.pallas_call(
        body,
        out_shape=[square] * outs,
        in_specs=[vmem] * len(blocks),
        out_specs=[vmem] * outs,
        scratch_shapes=[pltpu.VMEM((order, order), jnp.float32)] * 2 if solves else [],
        compiler_params=pltpu.CompilerParams(vmem_limit_bytes=12 * 2**20),
    )(*blocks)
    return list(results)


def first_step(marks, refl, trans, up, behind, c0, out0, down, solver, bounce, power, total):
    turned = marks()[0] == 1
    bounce[...] = product(jnp.where(turned, trans[...], up[...]), c0[...])

    def use(value):
        solver[...] = value
        down[...] = product(value, jnp.where(turned, up[...], trans[...]))
        out0[...] = refl[...] + product(bounce[...], down[...])

    solve(product(behind[...], c0[...]), use, power, total)


def first_rest(marks, trans, up, behind, solver, bounce, back, upward):
    turned = marks()[0] == 1
    back[...] = product(solver[...], behind[...])
    upward[...] = jnp.where(turned, trans[...], up[...]) + product(bounce[...], back[...])


def pick(marks, which, own, *rest):
    outs, sems = rest[:-1], rest[-1]
    turned = 2 * marks()[0]
    places = (turned, 1, 3, 2 - turned)
    copies = [pltpu.make_async_copy(own.at[places[i]], out, sems.at[n]) for n, (i, out) in enumerate(zip(which, outs))]
    for copy in copies:
        copy.start()
    for copy in copies:
        copy.wait()


def picked(marks, which, own):
    block = jax.ShapeDtypeStruct(own.shape[1:], jnp.float32)
    vmem = pl.BlockSpec(memory_space=pltpu.VMEM)
    return list(pl.pallas_call(
        functools.partial(pick, marks, which),
        out_shape=[block] * len(which),
        in_specs=[pl.BlockSpec(memory_space=pltpu.HBM)],
        out_specs=[vmem] * len(which),
        scratch_shapes=[pltpu.SemaphoreType.DMA((len(which),))],
        compiler_params=pltpu.CompilerParams(vmem_limit_bytes=12 * 2**20),
    )(pltpu.with_memory_space_constraint(own, pltpu.HBM)))


def second_step(marks, down, back, up, c1, out1, kept):
    turned = marks()[0] == 1
    out1[...] = product(jnp.where(turned, up[...], c1[...]), jnp.where(turned, c1[...], down[...]))
    kept[...] = product(jnp.where(turned, back[...], c1[...]), jnp.where(turned, c1[...], back[...]))


def third_step(marks, down, up, kept, c2, out2, rest):
    turned = marks()[0] == 1
    out2[...] = product(jnp.where(turned, c2[...], up[...]), jnp.where(turned, down[...], c2[...]))
    rest[...] = product(jnp.where(turned, c2[...], kept[...]), jnp.where(turned, kept[...], c2[...]))


def ordered(turned, first, last):
    return jnp.where(turned, last[...], first[...]), jnp.where(turned, first[...], last[...])


def lower_run(marks, o0, o1, o2, o3, refl_b, refl, down, power, total):
    refl_a, back_a = ordered(marks()[0] == 1, o0, o3)
    bounce = product(o2[...], refl_b[...])

    def use(value):
        down[...] = product(value, o1[...])
        refl[...] = refl_a + product(bounce, down[...])

    solve(product(back_a, refl_b[...]), use, power, total)


def upper_run(marks, o0, o1, o2, o3, c0, c1, c3, back, trans, solver, power, total):
    mark = marks()
    refl_b, back_b = ordered(mark[0] == 1, o0, o3)
    _, back_a = ordered(mark[1] == 1, c0, c3)
    turned_up = product(back_a, o2[...])

    def use(value):
        solver[...] = value
        through = product(o1[...], value)
        back[...] = back_b + product(through, turned_up)
        trans[...] = product(through, c1[...])

    solve(product(back_a, refl_b), use, power, total)


def whole_down(back_a, trans_a, refl_b, down, power, total):
    def use(value):
        down[...] = product(value, trans_a[...])

    solve(product(back_a[...], refl_b[...]), use, power, total)


def whole_refl(marks, o0, o2, o3, c0, c1, c2, c3, solver, low_refl, down, refl):
    mark = marks()
    refl_b, _ = ordered(mark[0] == 1, o0, o3)
    refl_a, back_a = ordered(mark[1] == 1, c0, c3)
    first = refl_a + product(c2[...], product(refl_b, product(solver[...], c1[...])))
    turned_up = product(solver[...], product(back_a, o2[...]))
    up = product(c2[...], o2[...] + product(refl_b, turned_up))
    refl[...] = first + product(up, product(low_refl[...], down[...]))


def any_run(marks, o0, o1, o2, o3, c0, c1, c2, c3, refl, trans, up, back, power, total):
    mark = marks()
    refl_own, back_own = ordered(mark[0] == 1, o0, o3)
    refl_came, back_came = ordered(mark[1] == 1, c0, c3)
    own, came = (refl_own, o1[...], o2[...], back_own), (refl_came, c1[...], c2[...], back_came)
    below = mark[2] == 1
    refl_a, trans_a, up_a, back_a = [jnp.where(below, c, o) for o, c in zip(own, came)]
    refl_b, trans_b, up_b, back_b = [jnp.where(below, o, c) for o, c in zip(own, came)]
    bounce = product(up_a, refl_b)

    def use(value):
        down = product(value, trans_a)
        turned_up = product(value, product(back_a, up_b))
        back[...] = back_b + product(trans_b, turned_up)
        trans[...] = product(trans_b, down)
        up[...] = product(up_a, up_b) + product(bounce, turned_up)
        refl[...] = refl_a + product(bounce, down)

    solve(product(back_a, refl_b), use, power, total)


def times(left, right, out):
    out[...] = product(left[...], right[...])


def times_transpose(rows, matrix):
    return lax.dot_general(
        rows, matrix, (((1,), (1,)), ((), ())), precision=lax.Precision.HIGH, preferred_element_type=jnp.float32
    )


def last_step(odd, even, refl, field_out, bounced_out, field, bounced, sems):
    field[...] = jnp.where(lax.axis_index("depth") % 2 == 1, odd[...], even[...])
    rows = pltpu.make_async_copy(field, field_out, sems.at[0])
    rows.start()
    half = field.shape[0] // 2
    matrix_high, matrix_low = split(refl[...])
    dot = functools.partial(
        lax.dot_general, dimension_numbers=(((1,), (1,)), ((), ())), preferred_element_type=jnp.float32
    )
    copies = []
    for i in range(2):
        part = pl.ds(i * half, half)
        high, low = split(field[part, :])
        bounced[part, :] = dot(high, matrix_high) + (dot(high, matrix_low) + dot(low, matrix_high))
        copies.append(pltpu.make_async_copy(bounced.at[part, :], bounced_out.at[part, :], sems.at[1 + i]))
        copies[-1].start()
    rows.wait()
    for copy in copies:
        copy.wait()


def finish(odd, even, refl):
    shape = jax.ShapeDtypeStruct(odd.shape, jnp.float32)
    vmem, hbm = pl.BlockSpec(memory_space=pltpu.VMEM), pl.BlockSpec(memory_space=pl.ANY)
    return pl.pallas_call(
        last_step,
        out_shape=[shape, shape],
        in_specs=[vmem] * 3,
        out_specs=[hbm, hbm],
        scratch_shapes=[pltpu.VMEM(odd.shape, jnp.float32)] * 2 + [pltpu.SemaphoreType.DMA((3,))],
        compiler_params=pltpu.CompilerParams(vmem_limit_bytes=12 * 2**20),
    )(odd, even, refl)


def filled(useful, groups, count):
    def mate(device):
        return (device[0] ^ 1, device[1])

    pairs = dict(useful)
    targets = set(pairs.values())
    devices = [(g, s) for g in range(groups) for s in range(count)]
    for device in devices:
        if device not in pairs and mate(device) not in targets:
            pairs[device] = mate(device)
    spare = set(devices) - set(pairs.values())
    for source, target in useful.items():
        if mate(target) not in pairs and mate(source) in spare:
            pairs[mate(target)] = mate(source)
            spare.discard(mate(source))
    return pairs


def shards(slabs, incident):
    groups, count = lax.axis_size("depth"), lax.axis_size("slab")
    group, place = lax.axis_index("depth"), lax.axis_index("slab")
    levels = count.bit_length() - 1
    parity = group % 2
    pair, side = place // 2, place % 2
    pairs = count // 2

    def send(block, useful, fill=True):
        route = filled(useful, groups, count) if fill else useful
        route = sorted((a[0] * count + a[1], b[0] * count + b[1]) for a, b in route.items())
        return lax.ppermute(block, AXES, route)

    def turn(g, k):
        return g % 2 if k < pairs - 1 else 0

    def home(g, k):
        return (g, 2 * k + turn(g, k))

    def guest(g, k):
        return (g, 2 * k + 1 - turn(g, k))

    turned = jnp.where(pair == pairs - 1, 0, parity)
    owners = [list(range(pairs))]
    merges = []
    while len(owners[-1]) > 1:
        now, kept = owners[-1], []
        merges.append([])
        for k in range(0, len(now), 2):
            below = len(now) > 2 and k // 2 % 2 == 0
            merges[-1].append((now[k], now[k + 1], True) if below else (now[k + 1], now[k], False))
            kept.append(merges[-1][-1][1])
        owners.append(kept)

    def routes(level, late=False):
        return {
            home(g, source): home(g, target)
            for source, target, below in merges[level - 1]
            if below or not late
            for g in range(groups)
        }

    def is_one(some):
        return functools.reduce(jnp.logical_or, [pair == k for k in some], False)

    def marks(level):
        odd, at = lax.axis_index("depth") % 2, lax.axis_index("slab") // 2

        def among(some):
            return functools.reduce(jnp.maximum, [(at == k).astype(jnp.int32) for k in some], jnp.int32(0))

        below = among([m[1] for m in merges[max(level, 1) - 1] if m[2]])
        if level > 1:
            return jnp.int32(0), jnp.int32(0), below
        return (1 - among([pairs - 1])) * odd, among([m[1] for m in merges[0] if m[0] < pairs - 1]) * odd, below

    own = slabs[0, 0]
    injected = incident[0]
    spread = {guest(g, k): home(g, k) for g in range(groups) for k in range(pairs)}
    spread_late = {guest(g, k): home(g, k) for g in range(groups) for k in range(pairs - 1)}
    first = functools.partial(marks, 1)
    mine = picked(first, (0,), own)
    later, _ = lax.optimization_barrier((own, mine[0]))
    mine += picked(first, (1, 2, 3), later)
    came = [send(block, spread if n < 2 else spread_late) for n, block in enumerate(mine)]
    split_level = levels - 2
    late = split_level == 1
    out0, down, solver, bounce = call(functools.partial(first_step, first), mine + came[:1], 4, True)
    sent = [send(out0, routes(1))]
    back, up = call(functools.partial(first_rest, first), mine[1:] + [solver, bounce], 2)
    out1, kept = call(functools.partial(second_step, first), [down, back, up, came[1]], 2)
    sent.append(send(out1, routes(1)))
    out2, rest = call(functools.partial(third_step, first), [down, up, kept, came[2]], 2)
    sent.append(send(out2, routes(1, late)))
    out3 = came[3] + rest
    sent.append(send(out3, routes(1, late)))
    state = [out0, out1, out2, out3]
    for level in range(1, split_level):
        state = call(functools.partial(any_run, functools.partial(marks, level)), state + sent, 4, True)
        late = level + 1 == split_level
        sent = [send(block, routes(level + 1, late and i > 1)) for i, block in enumerate(state)]

    top = routes(levels - 1)
    split_marks = functools.partial(marks, split_level)
    low_refl, low_down = call(functools.partial(lower_run, split_marks), state + sent[:1], 2, True)
    low_refl = send(low_refl, top)
    (low_trans,) = call(times, [sent[1], low_down], 1)
    low_trans = send(low_trans, top)
    back_a, trans_a, solver = call(functools.partial(upper_run, split_marks), state + [sent[0], sent[1], sent[3]], 3, True)
    back_a, _ = lax.optimization_barrier((back_a, sent[2]))
    (down,) = call(whole_down, [back_a, trans_a, low_refl], 1, True)
    (trans,) = call(times, [low_trans, down], 1)
    (refl,) = call(functools.partial(whole_refl, split_marks), [state[0], state[2], state[3]] + sent + [solver, low_refl, down], 1)

    def line(g, k):
        return (g, 2 * k + g % 2)

    def hand_out(block, fill, order, last=0):
        level = levels - 1
        while level > 0:
            steps = []
            for far, near, _ in merges[level - 1]:
                if level > 1:
                    below = {m[1]: m[0] for m in merges[level - 2]}
                    steps.append([[(near, below[far]), (near, far), (near, below[near])][n] for n in order])
                else:
                    steps.append([(near, far)])
            got = block
            for step, full in zip(zip(*steps), fill):
                fresh = is_one([target for _, target in step])
                route = {line(g, a): line(g, b) for a, b in step for g in range(groups - last)}
                got = jnp.where(fresh, send(block, route, full), got)
            block = got
            level -= 2
        return block

    trans, _ = lax.optimization_barrier((hand_out(trans, (True, True, True), (1, 0, 2), 1), refl))
    refl = hand_out(refl, (False, False, False), (0, 1, 2))

    across = {}
    for g in range(groups - 1):
        for k in range(pairs):
            across[line(g, k)] = (g | 1, 2 * k + 1 - g % 2)
    swap = {(g, s): (g ^ 1, s) for g in range(groups) for s in range(count)}
    even = send(injected, swap)
    crossed = send(trans, across, False)
    trans_even = jnp.where(side == 1, crossed, send(trans, swap))
    trans_odd = jnp.where(side == 1, trans, crossed)
    opposite = {line(g, k): (g, line(g, k)[1] ^ 1) for g in range(groups) for k in range(pairs)}
    spread_refl = jnp.where(side == parity, refl, send(refl, opposite))
    handed = jnp.zeros_like(injected)
    for j in range(0, groups, 2):
        field_even = even + handed
        field_odd = injected + times_transpose(field_even, trans_even)
        if j + 2 < groups:
            leaving, _ = lax.optimization_barrier((times_transpose(field_odd, trans_odd), refl))
            arriving = send(leaving, {(j + 1, s): (j + 3, s) for s in range(count)})
            arriving, _ = lax.optimization_barrier((arriving, spread_refl))
            handed = jnp.where(group // 2 == j // 2 + 1, arriving, handed)
    field, bounced = finish(field_odd, send(field_even, swap), spread_refl)
    return (field[None], bounced[None])


def solution(mesh):
    placed = (P("depth", "slab", None, None, None), P("depth", "slab", None))
    return jax.shard_map(
        shards,
        mesh=mesh,
        in_specs=placed,
        out_specs=(P("depth", "slab", None), P("depth", "slab", None)),
        check_vma=False,
    )
```
